32 devices in a mesh: row: 2 (over x), col: 16 (over z, y, core).
Axes of the slice: x: 2, y: 2, z: 4, core: 2. Of those that a mesh axis runs over, the one named last changes fastest.
Arguments:
- tokens: bfloat16 [128, 7168], P(('row', 'col')), may hold values from -6 to 6
- gate_up: bfloat16 [16, 2, 1536, 7168], P('col', None, 'row'), may hold values from -0.0625 to 0.0625
- down: bfloat16 [16, 1536, 7168], P('col', None, 'row'), may hold values from -0.15625 to 0.15625
- expert_ids: int32 [128, 8], replicated, may hold values from 0 to 15, all different within a row; in each aligned block of 64 rows (0 to 63, 64 to 127, ...) at most 48 rows name the same one
- gate_weights: float32 [128, 8], replicated, may hold values from 0.05 to 1
- capacity: int32 [16], replicated, may hold values from 24 to 48
Outputs:
- routed_out: bfloat16 [128, 7168], P(('row', 'col'))
The draws below stay inside these ranges and needn't reach their ends.
Inputs may be any that keep to these rules, and one draw needn't show every extreme that they name: `expert_ids`: each row names 8 different experts; within each aligned group of 64 rows no expert is named by more than 48 rows.
All inputs are finite; a program needn't handle non-finite values.
Results may differ from the reference program's by a relative error of at most 0.0063.
Values may be sent and summed in bfloat16 or wider, within the bound.
A program may use at most 64 MiB of HBM per device.

```python
import math
import jax
import jax.numpy as jnp
import numpy as np
from jax import lax

D = 7168
TOP = 8
MOE_H = 1536
TOK_DEV = 4
EXPERTS = 16
TOKENS = 128
RCAP = 48
N_ROW = 2
N_COL = 16


def draw_capacity(key, part):
    key = jax.random.fold_in(key, 7)
    value_key, pick_key = jax.random.split(key)
    values = jax.random.randint(value_key, (EXPERTS,), RCAP // 2, RCAP + 1)
    chosen = jax.random.randint(pick_key, (), 0, EXPERTS)
    return jnp.where(jnp.arange(EXPERTS) == chosen, RCAP, values).astype(jnp.int32)


def block_levels(own_key, shape, cuts, smallest, largest):
    level = 1.0
    for dim, shards_of in cuts:
        heights = jax.random.uniform(jax.random.fold_in(jax.random.fold_in(own_key, 6), dim), (shards_of,), jnp.float32, smallest / len(cuts), largest / len(cuts))
        level = level * jnp.repeat(jnp.exp(heights), shape[dim] // shards_of).reshape((-1,) + (1,) * (len(shape) - 1 - dim))
    return level


def deal_out(key, own, number, rows, number_of, top, most, lean):
    ranking = jax.random.permutation(key, number_of)
    packed, usual = load_shares(number_of, rows * top, most, lean, True), load_shares(number_of, rows * top, most, lean, False)
    places = jnp.arange(number_of)

    def named(sizes, rotation):
        used = int((sizes > 0).sum())
        fixed = max(1, used // 4)
        moved = fixed + (places - fixed + rotation * (used - fixed)) % max(1, number_of - fixed)
        return jnp.zeros((number_of,), jnp.int32).at[ranking[jnp.where(places < fixed, places, moved)]].set(jnp.asarray(sizes, jnp.int32))

    sizes = jnp.where(number % 4 == 0, named(packed, number // 4), named(usual, number - number // 4 - 1))
    mixed = jax.random.permutation(jax.random.fold_in(own, 3), number_of)
    source_of, taker = mixed[0:number_of // 2 * 2:2], mixed[1:number_of // 2 * 2:2]
    room = jnp.minimum(sizes[source_of] - 1, most - sizes[taker]) // 2
    room = jnp.where((source_of == ranking[0]) | (taker == ranking[0]) | (sizes[taker] == 0), 0, jnp.maximum(room, 0))
    moved = jax.random.randint(jax.random.fold_in(own, 4), (number_of // 2,), 0, 1 << 20) % (room + 1)
    sizes = sizes.at[source_of].add(-moved).at[taker].add(moved)
    items = jnp.searchsorted(jnp.cumsum(sizes), jnp.arange(rows * top), side="right").astype(jnp.int32)
    grid = items.reshape(top, rows).T
    grid = grid[jax.random.permutation(jax.random.fold_in(own, 1), rows)]
    rotation = jax.random.randint(jax.random.fold_in(own, 2), (rows, 1), 0, top)
    return jnp.take_along_axis(grid, (jnp.arange(top)[None, :] + rotation) % top, axis=1)


def load_shares(number_of, total, most, lean, full):
    weights = [(1 << 20) // math.isqrt(grade ** lean) + 1 for grade in range(1, number_of + 1)]
    largest = most if full else min(most, max(-(-total // number_of), total * weights[0] // sum(weights)))
    least = 1 if total - largest >= number_of - 1 else 0
    given, spare = [largest] + [least] * (number_of - 1), total - largest - least * (number_of - 1)
    while spare > 0:
        candidates = [i for i in range(1, number_of) if given[i] < largest] or [i for i in range(1, number_of) if given[i] < most]
        whole, budget = sum([weights[i] for i in candidates]), spare
        for i in candidates:
            more = min(most - given[i], max(1, budget * weights[i] // whole), spare)
            given[i] = given[i] + more
            spare = spare - more
    return np.array(given)


def gaussian(own_key, dims, deviation, limit, shards=(), kind=jnp.bfloat16):
    array = deviation * jax.random.normal(own_key, dims, jnp.float32)
    if shards:
        array = array * block_levels(own_key, dims, shards, -0.22, 0.18)
    return jnp.clip(array, -limit, limit).astype(kind)


def setup_inputs(seed: int = 0) -> dict:
    arg_keys = jax.random.split(jax.random.key(seed), 7)
    tokens = gaussian(arg_keys[0], (TOKENS, D), 1.0, 6.0, ((0, 32),))
    gate_up = gaussian(arg_keys[1], (EXPERTS, 2, MOE_H, D), D ** -0.5, 0.0625, ((0, 16), (2, 2)))
    down = gaussian(arg_keys[2], (EXPERTS, MOE_H, D), MOE_H ** -0.5, 0.15625, ((0, 16), (2, 2)))
    expert_ids_keys = jax.random.split(jax.random.fold_in(arg_keys[3], 1), TOKENS // (N_COL * TOK_DEV))
    expert_ids_turns = jax.random.permutation(jax.random.fold_in(arg_keys[3], 3), TOKENS // (N_COL * TOK_DEV))
    expert_ids = jax.vmap(lambda own, number: deal_out(jax.random.fold_in(arg_keys[3], 2), own, number, N_COL * TOK_DEV, EXPERTS, TOP, RCAP, 2))(expert_ids_keys, expert_ids_turns).reshape((TOKENS, TOP))
    gate_weights = jnp.clip(jnp.exp(jax.random.uniform(arg_keys[4], (TOKENS, TOP), jnp.float32, math.log(0.05), math.log(1.0))), 0.05, 1.0)
    capacity = draw_capacity(jax.random.fold_in(arg_keys[6], 71), 0)
    return {"tokens": tokens, "gate_up": gate_up, "down": down, "expert_ids": expert_ids, "gate_weights": gate_weights, "capacity": capacity}


def expert_slots(expert_ids, gate_weights, capacity, expert):
    total_rows = expert_ids.shape[0]
    block_rows = N_COL * TOK_DEV
    member = expert_ids == expert
    hit_count = jnp.sum(member.astype(jnp.int32), axis=1).astype(jnp.int32)
    grouped = hit_count.reshape(total_rows // block_rows, block_rows)
    rank_in = (jnp.cumsum(grouped, axis=1).astype(jnp.int32) - grouped).reshape(total_rows)
    cap_here = lax.dynamic_index_in_dim(capacity, expert, 0, keepdims=False)
    usable = (hit_count > 0) & (rank_in < cap_here)
    weights = jnp.sum(jnp.where(member, gate_weights, 0.0), axis=1)
    groups = jnp.arange(total_rows, dtype=jnp.int32) // block_rows
    slot_ids = jnp.where(usable, groups * RCAP + rank_in, -1).astype(jnp.int32)
    return slot_ids, weights


def reference(tokens, gate_up, down, expert_ids, gate_weights, capacity):
    slot_count = N_ROW * RCAP
    slot_index = jnp.arange(slot_count, dtype=jnp.int32)

    def one_expert(running, inputs):
        weights_gu, weights_down, expert = inputs
        slot_ids, weights = expert_slots(expert_ids, gate_weights, capacity, expert)
        select = (slot_index[:, None] == slot_ids[None, :]).astype(jnp.bfloat16)
        picked = jnp.dot(select, tokens, preferred_element_type=jnp.float32).astype(jnp.bfloat16)
        gate_part = jnp.dot(picked, weights_gu[0].T, preferred_element_type=jnp.float32)
        up_part = jnp.dot(picked, weights_gu[1].T, preferred_element_type=jnp.float32)
        hidden = (jax.nn.silu(gate_part) * up_part).astype(jnp.bfloat16)
        outputs = jnp.dot(hidden, weights_down, preferred_element_type=jnp.float32).astype(jnp.bfloat16)
        combine = jnp.where(slot_ids[:, None] == slot_index[None, :], weights[:, None], 0.0).astype(jnp.bfloat16)
        return running + jnp.dot(combine, outputs, preferred_element_type=jnp.float32), None

    initial = jnp.zeros(tokens.shape, jnp.float32)
    summed, unused = lax.scan(one_expert, initial, (gate_up, down, jnp.arange(EXPERTS, dtype=jnp.int32)))
    return summed.astype(jnp.bfloat16)
```

```python
import functools

import jax
import jax.numpy as jnp
from jax import lax
from jax.experimental import pallas as pl
from jax.experimental.pallas import tpu as pltpu
from jax.sharding import PartitionSpec as P

TOP = 8
MESH = pl.DeviceIdType.MESH
CORES, YS, ZS, ROWS = 2, 2, 4, 2
TILE = 256


def fused_kernel(
    nk,
    nr,
    tokens_ref,
    ids_ref,
    weights_ref,
    capacity_ref,
    gate_up_ref,
    down_ref,
    out_ref,
    wgu,
    wd,
    xbuf,
    x2d,
    acc,
    hid,
    yacc,
    zf,
    r1_out,
    r1_in,
    p1,
    r2_out,
    r2_in,
    p2,
    r3_out,
    r3_in,
    p3,
    r4_in,
    load_sem,
    g_send,
    g_recv,
    h_send,
    h_recv,
    r_send,
    r_recv,
):
    row = lax.axis_index("row")
    col = lax.axis_index("col")
    core = col % CORES
    y = (col // CORES) % YS
    z = col // (CORES * YS)
    tok_dev, width = tokens_ref.shape
    kc = width // nk
    tokens = x2d.shape[1]
    half = down_ref.shape[2]
    nc = half // nr
    hidden = gate_up_ref.shape[2]
    tiles = hidden // TILE

    x_peer = (1 - row, col)
    y_peer = (row, z * 4 + (1 - y) * 2 + core)
    core_peer = (row, z * 4 + y * 2 + 1 - core)
    z_places = (z + 1 - 2 * (z % 2), (z + 2) % ZS, ZS - 1 - z)
    z_peers = [(row, place * 4 + y * 2 + core) for place in z_places]

    def load_gu(k):
        columns = pl.ds(k * kc, kc)
        return pltpu.make_async_copy(
            gate_up_ref.at[0, :, :, columns], wgu.at[:, :, columns], load_sem.at[k]
        )

    def load_d(n):
        columns = pl.ds(n * nc, nc)
        return pltpu.make_async_copy(
            down_ref.at[0, :, columns], wd.at[:, columns], load_sem.at[nk + n]
        )

    for k in range(nk):
        load_gu(k).start()
    for n in range(nr):
        load_d(n).start()

    barrier = pltpu.get_barrier_semaphore()
    for peer in [x_peer, y_peer, core_peer] + z_peers:
        pl.semaphore_signal(barrier, inc=1, device_id=peer, device_id_type=MESH)
    for k in range(nk):
        xbuf[k, core, y, z, row] = tokens_ref[:, k * kc : (k + 1) * kc]
    pl.semaphore_wait(barrier, 6)

    def remote(src, dst, send, recv, peer):
        return pltpu.make_async_remote_copy(
            src_ref=src,
            dst_ref=dst,
            send_sem=send,
            recv_sem=recv,
            device_id=peer,
            device_id_type=MESH,
        )

    def gather(k, index, part, peer):
        return remote(part, part, g_send.at[k, index], g_recv.at[k, index], peer)

    def gather_1(k):
        part = xbuf.at[k, core, y, z, row]
        return [gather(k, 0, part, x_peer if k % 2 == 0 else y_peer)]

    def gather_2(k):
        part = xbuf.at[k, core, y, z] if k % 2 == 0 else xbuf.at[k, core, :, z, row]
        return [gather(k, 1 + i, part, z_peers[i]) for i in range(ZS - 1)]

    def gather_3(k):
        if k % 2 == 0:
            return [gather(k, 4, xbuf.at[k, core, y], y_peer)]
        return [gather(k, 4, xbuf.at[k, core, :, :, row], x_peer)]

    def gather_4(k):
        return [gather(k, 5, xbuf.at[k, core], core_peer)]

    started = []

    def start(copies):
        for copy in copies:
            copy.start()
            started.append(copy)

    def arrived(copies):
        for copy in copies:
            copy.wait_recv()

    for k in range(nk):
        start(gather_1(k))
    for k in range(nk):
        arrived(gather_1(k))
        start(gather_2(k))
    for k in range(nk):
        arrived(gather_2(k))
        start(gather_3(k))

    member = ids_ref[...] == col
    hit_row = jnp.sum(member.astype(jnp.float32), axis=0, keepdims=True)
    weight_row = jnp.sum(jnp.where(member, weights_ref[...], 0.0), axis=0, keepdims=True)
    place = lax.broadcasted_iota(jnp.int32, (tokens, tokens), 0)
    other = lax.broadcasted_iota(jnp.int32, (tokens, tokens), 1)
    group = tokens // ROWS
    token = (
        ((place // 4) % 2) * group
        + ((place // 8) % 4) * 16
        + ((place // 32) % 2) * 8
        + (place // 64) * 4
        + place % 4
    )
    earlier = (other < token) & (other // group == token // group)
    rank = jnp.sum(jnp.where(earlier, hit_row, 0.0), axis=1, keepdims=True)
    same = other == token
    hit = jnp.sum(jnp.where(same, hit_row, 0.0), axis=1, keepdims=True)
    weight = jnp.sum(jnp.where(same, weight_row, 0.0), axis=1, keepdims=True)
    limit = capacity_ref[col].astype(jnp.float32)
    combine = jnp.where((hit > 0.5) & (rank < limit), weight, 0.0)
    combine = combine.astype(jnp.bfloat16).astype(jnp.float32)

    def pass_on(k):
        arrived(gather_3(k))
        start(gather_4(k))

    def send_hidden(h):
        part = hid.at[row, h]
        return [remote(part, part, h_send.at[h], h_recv.at[h], x_peer)]

    def product(k, part, h):
        return lax.dot_general(
            x2d[k],
            wgu[part, h * TILE : (h + 1) * TILE, k * kc : (k + 1) * kc],
            (((1,), (1,)), ((), ())),
            preferred_element_type=jnp.float32,
        )

    pass_on(0)
    for k in range(nk):
        if k + 1 < nk:
            pass_on(k + 1)
        arrived(gather_4(k))
        block = xbuf[k].reshape(tokens // tok_dev, tok_dev, kc).astype(jnp.float32)
        x2d[k] = block.reshape(tokens, kc).astype(jnp.bfloat16)
        load_gu(k).wait()
        for h in range(tiles):
            gate = product(k, 0, h)
            up = product(k, 1, h)
            if k > 0:
                gate = gate + acc[0, h]
                up = up + acc[1, h]
            if k < nk - 1:
                acc[0, h] = gate
                acc[1, h] = up
            else:
                hid[row, h] = (gate / (1.0 + jnp.exp(-gate)) * up).astype(jnp.bfloat16)
                start(send_hidden(h))

    def down_part(n, side):
        total = None
        for h in range(tiles):
            rows = pl.ds(pl.multiple_of(side * hidden + h * TILE, TILE), TILE)
            term = jnp.dot(
                hid[side, h],
                wd[rows, n * nc : (n + 1) * nc],
                preferred_element_type=jnp.float32,
            )
            total = term if total is None else total + term
        return total

    def reduce_1(n):
        return [remote(r1_out.at[n], r1_in.at[n], r_send.at[n, 0], r_recv.at[n, 0], core_peer)]

    def reduce_2(n):
        return [remote(r2_out.at[n], r2_in.at[n], r_send.at[n, 1], r_recv.at[n, 1], y_peer)]

    def reduce_3(n):
        return [
            remote(
                r3_out.at[n, z_places[i]],
                r3_in.at[n, i],
                r_send.at[n, 2 + i],
                r_recv.at[n, 2 + i],
                z_peers[i],
            )
            for i in range(ZS - 1)
        ]

    def reduce_4(n):
        return [
            remote(p3.at[n, 1 - row], r4_in.at[n], r_send.at[n, 5], r_recv.at[n, 5], x_peer)
        ]

    def after_core(n):
        arrived(reduce_1(n))
        both = zf[n, core] + r1_in[n].astype(jnp.float32)
        p1[n] = both.reshape(p1.shape[1:])
        r2_out[n] = p1[n, 1 - y].astype(jnp.bfloat16)
        start(reduce_2(n))

    def after_y(n):
        arrived(reduce_2(n))
        both = p1[n, y] + r2_in[n].astype(jnp.float32)
        p2[n] = both.reshape(p2.shape[1:])
        r3_out[n] = p2[n].astype(jnp.bfloat16)
        start(reduce_3(n))

    def after_z(n):
        arrived(reduce_3(n))
        total = p2[n, z]
        for i in range(ZS - 1):
            total = total + r3_in[n, i].astype(jnp.float32)
        p3[n, 0] = total[:tok_dev].astype(jnp.bfloat16)
        p3[n, 1] = total[tok_dev:].astype(jnp.bfloat16)
        start(reduce_4(n))

    for n in range(nr):
        load_d(n).wait()
        yacc[n] = down_part(n, row)
    for h in range(tiles):
        arrived(send_hidden(h))
    for n in range(nr + 2):
        if n < nr:
            total = (yacc[n] + down_part(n, 1 - row)).astype(jnp.bfloat16)
            scaled = total.astype(jnp.float32) * combine
            zf[n] = scaled.reshape(zf.shape[1:])
            r1_out[n] = zf[n, 1 - core].astype(jnp.bfloat16)
            start(reduce_1(n))
        if 1 <= n <= nr:
            after_core(n - 1)
        if n >= 2:
            after_y(n - 2)
    for n in range(nr):
        after_z(n)
    for n in range(nr):
        mine = pl.ds(pl.multiple_of(row * half + n * nc, 128), nc)
        theirs = pl.ds(pl.multiple_of((1 - row) * half + n * nc, 128), nc)
        out_ref[:, mine] = p3[n, row]
        arrived(reduce_4(n))
        out_ref[:, theirs] = r4_in[n]
    for copy in started:
        copy.wait_send()


def fused(tokens, gate_up, down, expert_ids, gate_weights, capacity):
    nk, nr = 4, 4
    tok_dev, width = tokens.shape
    total = expert_ids.shape[0]
    hidden = gate_up.shape[2]
    half = down.shape[2]
    kc, nc = width // nk, half // nr
    tiles = hidden // TILE
    vmem = pl.BlockSpec(memory_space=pltpu.VMEM)
    hbm = pl.BlockSpec(memory_space=pl.ANY)
    bf16, f32 = jnp.bfloat16, jnp.float32
    per_core, per_y, per_z = total // CORES, total // (CORES * YS), total // (CORES * YS * ZS)
    dma = pltpu.SemaphoreType.DMA
    return pl.pallas_call(
        functools.partial(fused_kernel, nk, nr),
        out_shape=jax.ShapeDtypeStruct(tokens.shape, bf16),
        in_specs=[vmem, vmem, vmem, pl.BlockSpec(memory_space=pltpu.SMEM), hbm, hbm],
        out_specs=vmem,
        scratch_shapes=[
            pltpu.VMEM((2, hidden, width), bf16),
            pltpu.VMEM((ROWS * hidden, half), bf16),
            pltpu.VMEM((nk, CORES, YS, ZS, ROWS, tok_dev, kc), bf16),
            pltpu.VMEM((nk, total, kc), bf16),
            pltpu.VMEM((2, tiles, total, TILE), f32),
            pltpu.VMEM((ROWS, tiles, total, TILE), bf16),
            pltpu.VMEM((nr, total, nc), f32),
            pltpu.VMEM((nr, CORES, per_core, nc), f32),
            pltpu.VMEM((nr, per_core, nc), bf16),
            pltpu.VMEM((nr, per_core, nc), bf16),
            pltpu.VMEM((nr, YS, per_y, nc), f32),
            pltpu.VMEM((nr, per_y, nc), bf16),
            pltpu.VMEM((nr, per_y, nc), bf16),
            pltpu.VMEM((nr, ZS, per_z, nc), f32),
            pltpu.VMEM((nr, ZS, per_z, nc), bf16),
            pltpu.VMEM((nr, ZS - 1, per_z, nc), bf16),
            pltpu.VMEM((nr, ROWS, tok_dev, nc), bf16),
            pltpu.VMEM((nr, tok_dev, nc), bf16),
            dma((nk + nr,)),
            dma((nk, 6)),
            dma((nk, 6)),
            dma((tiles,)),
            dma((tiles,)),
            dma((nr, 6)),
            dma((nr, 6)),
        ],
        compiler_params=pltpu.CompilerParams(
            collective_id=0, has_side_effects=True, vmem_limit_bytes=56 * 1024 * 1024
        ),
        cost_estimate=pl.CostEstimate(
            flops=6 * total * hidden * width,
            bytes_accessed=2 * (gate_up.size + down.size),
            transcendentals=total * hidden,
        ),
    )(tokens, expert_ids.T, gate_weights.T, capacity, gate_up, down)


def expert_slots(expert_ids, gate_weights, capacity, expert, block_rows, slot_cap):
    total_rows = expert_ids.shape[0]
    member = expert_ids == expert
    hit_count = jnp.sum(member.astype(jnp.int32), axis=1)
    grouped = hit_count.reshape(total_rows // block_rows, block_rows)
    rank_in = (jnp.cumsum(grouped, axis=1) - grouped).reshape(total_rows)
    cap_here = lax.dynamic_index_in_dim(capacity, expert, 0, keepdims=False)
    usable = (hit_count > 0) & (rank_in < cap_here)
    weights = jnp.sum(jnp.where(member, gate_weights, 0.0), axis=1)
    groups = jnp.arange(total_rows, dtype=jnp.int32) // block_rows
    slot_ids = jnp.where(usable, groups * slot_cap + rank_in, -1)
    return (slot_ids, weights)


def local(tokens, gate_up, down, expert_ids, gate_weights, capacity):
    col_count = lax.axis_size("col")
    row_count = lax.axis_size("row")
    col_index = lax.axis_index("col")
    row_index = lax.axis_index("row")
    tok_dev = tokens.shape[0]
    block_rows = col_count * tok_dev
    slot_cap = min(3 * tok_dev * TOP // 2, block_rows)
    slot_count = row_count * slot_cap
    total_rows = expert_ids.shape[0]
    slot_ids, weights = expert_slots(
        expert_ids, gate_weights, capacity, col_index, block_rows, slot_cap
    )
    group_tokens = lax.all_gather(tokens, "col", axis=0, tiled=True)
    local_slots = (
        lax.dynamic_slice_in_dim(slot_ids, row_index * block_rows, block_rows)
        - row_index * slot_cap
    )
    cap_index = jnp.arange(slot_cap, dtype=jnp.int32)
    select = (cap_index[:, None] == local_slots[None, :]).astype(jnp.bfloat16)
    picked = jnp.dot(select, group_tokens, preferred_element_type=jnp.float32).astype(jnp.bfloat16)
    w_gate = gate_up[0, 0]
    w_up = gate_up[0, 1]
    contract = (((1,), (1,)), ((), ()))
    piece = lax.all_gather(picked, "row", axis=0, tiled=True)
    gate_part = lax.dot_general(piece, w_gate, contract, preferred_element_type=jnp.float32)
    up_part = lax.dot_general(piece, w_up, contract, preferred_element_type=jnp.float32)
    hidden = (jax.nn.silu(gate_part) * up_part).astype(jnp.bfloat16)
    w_down = down[0]
    outputs = jnp.dot(
        lax.all_gather(hidden, "row", axis=1, tiled=True),
        w_down,
        preferred_element_type=jnp.float32,
    ).astype(jnp.bfloat16)

    def by_column(values):
        return values.reshape(row_count, col_count, tok_dev).transpose(1, 0, 2).reshape(total_rows)

    column_slots = by_column(slot_ids)
    column_weights = by_column(weights)
    slot_index = jnp.arange(slot_count, dtype=jnp.int32)
    combine = jnp.where(
        column_slots[:, None] == slot_index[None, :], column_weights[:, None], 0.0
    ).astype(jnp.bfloat16)
    summed = lax.psum_scatter(
        jnp.dot(combine, outputs, preferred_element_type=jnp.float32),
        "col",
        scatter_dimension=0,
        tiled=True,
    )
    own_rows = lax.all_to_all(
        summed.astype(jnp.bfloat16), "row", split_axis=0, concat_axis=1, tiled=True
    ).astype(summed.dtype)
    return own_rows.astype(jnp.bfloat16)


def solution(mesh):
    in_specs = (
        P(("row", "col"), None),
        P("col", None, "row", None),
        P("col", None, "row"),
        P(),
        P(),
        P(),
    )
    out_specs = P(("row", "col"), None)
    small = mesh.shape["row"] == ROWS and mesh.shape["col"] == CORES * YS * ZS
    return jax.shard_map(
        fused if small else local, mesh=mesh, in_specs=in_specs, out_specs=out_specs, check_vma=False
    )
```

```python
import functools

import jax
import jax.numpy as jnp
from jax import lax
from jax.experimental import pallas as pl
from jax.experimental.pallas import tpu as pltpu
from jax.sharding import PartitionSpec as P

TOP = 8
MESH = pl.DeviceIdType.MESH
CORES, YS, ZS, ROWS = 2, 2, 4, 2
TILE = 256


def fused_kernel(
    nk,
    nr,
    tokens_ref,
    ids_ref,
    weights_ref,
    capacity_ref,
    gate_up_ref,
    down_ref,
    out_ref,
    wgu,
    wd,
    xbuf,
    x2d,
    acc,
    hid,
    yacc,
    zf,
    r1_out,
    r1_in,
    p1,
    r2_out,
    r2_in,
    p2,
    r3_out,
    r3_in,
    p3,
    r4_in,
    load_sem,
    g_send,
    g_recv,
    h_send,
    h_recv,
    r_send,
    r_recv,
):
    row = lax.axis_index("row")
    col = lax.axis_index("col")
    core = col % CORES
    y = (col // CORES) % YS
    z = col // (CORES * YS)
    tok_dev, width = tokens_ref.shape
    kc = width // nk
    tokens = x2d.shape[1]
    half = down_ref.shape[2]
    nc = half // nr
    hidden = gate_up_ref.shape[2]
    tiles = hidden // TILE

    x_peer = (1 - row, col)
    y_peer = (row, z * 4 + (1 - y) * 2 + core)
    core_peer = (row, z * 4 + y * 2 + 1 - core)
    z_places = (z + 1 - 2 * (z % 2), (z + 2) % ZS, ZS - 1 - z)
    z_peers = [(row, place * 4 + y * 2 + core) for place in z_places]

    def load_gu(k):
        columns = pl.ds(k * kc, kc)
        return pltpu.make_async_copy(
            gate_up_ref.at[0, :, :, columns], wgu.at[:, :, columns], load_sem.at[k]
        )

    def load_d(n):
        columns = pl.ds(n * nc, nc)
        return pltpu.make_async_copy(
            down_ref.at[0, :, columns], wd.at[:, columns], load_sem.at[nk + n]
        )

    for k in range(nk):
        load_gu(k).start()
    for n in range(nr):
        load_d(n).start()

    barrier = pltpu.get_barrier_semaphore()
    for peer in [x_peer, y_peer, core_peer] + z_peers:
        pl.semaphore_signal(barrier, inc=1, device_id=peer, device_id_type=MESH)
    for k in range(nk):
        xbuf[k, core, y, z, row] = tokens_ref[:, k * kc : (k + 1) * kc]
    pl.semaphore_wait(barrier, 6)

    def remote(src, dst, send, recv, peer):
        return pltpu.make_async_remote_copy(
            src_ref=src,
            dst_ref=dst,
            send_sem=send,
            recv_sem=recv,
            device_id=peer,
            device_id_type=MESH,
        )

    def gather(k, index, part, peer):
        return remote(part, part, g_send.at[k, index], g_recv.at[k, index], peer)

    def gather_1(k):
        part = xbuf.at[k, core, y, z, row]
        return [gather(k, 0, part, x_peer if k % 2 == 0 else y_peer)]

    def gather_2(k):
        part = xbuf.at[k, core, y, z] if k % 2 == 0 else xbuf.at[k, core, :, z, row]
        return [gather(k, 1 + i, part, z_peers[i]) for i in range(ZS - 1)]

    def gather_3(k):
        if k % 2 == 0:
            return [gather(k, 4, xbuf.at[k, core, y], y_peer)]
        return [gather(k, 4, xbuf.at[k, core, :, :, row], x_peer)]

    def gather_4(k):
        return [gather(k, 5, xbuf.at[k, core], core_peer)]

    started = []

    def start(copies):
        for copy in copies:
            copy.start()
            started.append(copy)

    def arrived(copies):
        for copy in copies:
            copy.wait_recv()

    for k in range(nk):
        start(gather_1(k))
    for k in range(nk):
        arrived(gather_1(k))
        start(gather_2(k))
    for k in range(nk):
        arrived(gather_2(k))
        start(gather_3(k))

    member = ids_ref[...] == col
    hit_row = jnp.sum(member.astype(jnp.float32), axis=0, keepdims=True)
    weight_row = jnp.sum(jnp.where(member, weights_ref[...], 0.0), axis=0, keepdims=True)
    place = lax.broadcasted_iota(jnp.int32, (tokens, tokens), 0)
    other = lax.broadcasted_iota(jnp.int32, (tokens, tokens), 1)
    group = tokens // ROWS
    token = (
        ((place // 4) % 2) * group
        + ((place // 8) % 4) * 16
        + ((place // 32) % 2) * 8
        + (place // 64) * 4
        + place % 4
    )
    earlier = (other < token) & (other // group == token // group)
    rank = jnp.sum(jnp.where(earlier, hit_row, 0.0), axis=1, keepdims=True)
    same = other == token
    hit = jnp.sum(jnp.where(same, hit_row, 0.0), axis=1, keepdims=True)
    weight = jnp.sum(jnp.where(same, weight_row, 0.0), axis=1, keepdims=True)
    limit = capacity_ref[col].astype(jnp.float32)
    combine = jnp.where((hit > 0.5) & (rank < limit), weight, 0.0)
    combine = combine.astype(jnp.bfloat16).astype(jnp.float32)

    def pass_on(k):
        arrived(gather_3(k))
        start(gather_4(k))

    def send_hidden(h):
        part = hid.at[row, h]
        return [remote(part, part, h_send.at[h], h_recv.at[h], x_peer)]

    def product(k, part, first, count):
        return lax.dot_general(
            wgu[part, first : first + count, k * kc : (k + 1) * kc],
            x2d[k],
            (((1,), (1,)), ((), ())),
            preferred_element_type=jnp.float32,
        )

    pass_on(0)
    for k in range(nk):
        if k + 1 < nk:
            pass_on(k + 1)
        arrived(gather_4(k))
        block = xbuf[k].reshape(tokens // tok_dev, tok_dev, kc).astype(jnp.float32)
        x2d[k] = block.reshape(tokens, kc).astype(jnp.bfloat16)
        load_gu(k).wait()
        if k < nk - 1:
            for part in range(2):
                term = product(k, part, 0, hidden)
                acc[part] = term if k == 0 else acc[part] + term
            continue
        for h in range(tiles):
            rows = slice(h * TILE, (h + 1) * TILE)
            gate = acc[0, rows] + product(k, 0, h * TILE, TILE)
            up = acc[1, rows] + product(k, 1, h * TILE, TILE)
            act = gate / (1.0 + jnp.exp(-gate)) * up
            hid[row, h] = act.T.astype(jnp.bfloat16)
            start(send_hidden(h))

    def down_part(n, side):
        total = None
        for h in range(tiles):
            rows = pl.ds(pl.multiple_of(side * hidden + h * TILE, TILE), TILE)
            term = jnp.dot(
                hid[side, h],
                wd[rows, n * nc : (n + 1) * nc],
                preferred_element_type=jnp.float32,
            )
            total = term if total is None else total + term
        return total

    def reduce_1(n):
        return [remote(r1_out.at[n], r1_in.at[n], r_send.at[n, 0], r_recv.at[n, 0], core_peer)]

    def reduce_2(n):
        return [remote(r2_out.at[n], r2_in.at[n], r_send.at[n, 1], r_recv.at[n, 1], y_peer)]

    def reduce_3(n):
        return [
            remote(
                r3_out.at[n, z_places[i]],
                r3_in.at[n, i],
                r_send.at[n, 2 + i],
                r_recv.at[n, 2 + i],
                z_peers[i],
            )
            for i in range(ZS - 1)
        ]

    def reduce_4(n):
        return [
            remote(p3.at[n, 1 - row], r4_in.at[n], r_send.at[n, 5], r_recv.at[n, 5], x_peer)
        ]

    def after_core(n):
        arrived(reduce_1(n))
        both = zf[n, core] + r1_in[n].astype(jnp.float32)
        p1[n] = both.reshape(p1.shape[1:])
        r2_out[n] = p1[n, 1 - y].astype(jnp.bfloat16)
        start(reduce_2(n))

    def after_y(n):
        arrived(reduce_2(n))
        both = p1[n, y] + r2_in[n].astype(jnp.float32)
        p2[n] = both.reshape(p2.shape[1:])
        r3_out[n] = p2[n].astype(jnp.bfloat16)
        start(reduce_3(n))

    def after_z(n):
        arrived(reduce_3(n))
        total = p2[n, z]
        for i in range(ZS - 1):
            total = total + r3_in[n, i].astype(jnp.float32)
        p3[n, 0] = total[:tok_dev].astype(jnp.bfloat16)
        p3[n, 1] = total[tok_dev:].astype(jnp.bfloat16)
        start(reduce_4(n))

    for n in range(nr):
        load_d(n).wait()
        yacc[n] = down_part(n, row)
    for h in range(tiles):
        arrived(send_hidden(h))
    for n in range(nr + 2):
        if n < nr:
            total = (yacc[n] + down_part(n, 1 - row)).astype(jnp.bfloat16)
            scaled = total.astype(jnp.float32) * combine
            zf[n] = scaled.reshape(zf.shape[1:])
            r1_out[n] = zf[n, 1 - core].astype(jnp.bfloat16)
            start(reduce_1(n))
        if 1 <= n <= nr:
            after_core(n - 1)
        if n >= 2:
            after_y(n - 2)
    for n in range(nr):
        after_z(n)
    for n in range(nr):
        mine = pl.ds(pl.multiple_of(row * half + n * nc, 128), nc)
        theirs = pl.ds(pl.multiple_of((1 - row) * half + n * nc, 128), nc)
        out_ref[:, mine] = p3[n, row]
        arrived(reduce_4(n))
        out_ref[:, theirs] = r4_in[n]
    for copy in started:
        copy.wait_send()


def fused(tokens, gate_up, down, expert_ids, gate_weights, capacity):
    nk, nr = 4, 4
    tok_dev, width = tokens.shape
    total = expert_ids.shape[0]
    hidden = gate_up.shape[2]
    half = down.shape[2]
    kc, nc = width // nk, half // nr
    tiles = hidden // TILE
    vmem = pl.BlockSpec(memory_space=pltpu.VMEM)
    hbm = pl.BlockSpec(memory_space=pl.ANY)
    bf16, f32 = jnp.bfloat16, jnp.float32
    per_core, per_y, per_z = total // CORES, total // (CORES * YS), total // (CORES * YS * ZS)
    dma = pltpu.SemaphoreType.DMA
    return pl.pallas_call(
        functools.partial(fused_kernel, nk, nr),
        out_shape=jax.ShapeDtypeStruct(tokens.shape, bf16),
        in_specs=[vmem, vmem, vmem, pl.BlockSpec(memory_space=pltpu.SMEM), hbm, hbm],
        out_specs=vmem,
        scratch_shapes=[
            pltpu.VMEM((2, hidden, width), bf16),
            pltpu.VMEM((ROWS * hidden, half), bf16),
            pltpu.VMEM((nk, CORES, YS, ZS, ROWS, tok_dev, kc), bf16),
            pltpu.VMEM((nk, total, kc), bf16),
            pltpu.VMEM((2, hidden, total), f32),
            pltpu.VMEM((ROWS, tiles, total, TILE), bf16),
            pltpu.VMEM((nr, total, nc), f32),
            pltpu.VMEM((nr, CORES, per_core, nc), f32),
            pltpu.VMEM((nr, per_core, nc), bf16),
            pltpu.VMEM((nr, per_core, nc), bf16),
            pltpu.VMEM((nr, YS, per_y, nc), f32),
            pltpu.VMEM((nr, per_y, nc), bf16),
            pltpu.VMEM((nr, per_y, nc), bf16),
            pltpu.VMEM((nr, ZS, per_z, nc), f32),
            pltpu.VMEM((nr, ZS, per_z, nc), bf16),
            pltpu.VMEM((nr, ZS - 1, per_z, nc), bf16),
            pltpu.VMEM((nr, ROWS, tok_dev, nc), bf16),
            pltpu.VMEM((nr, tok_dev, nc), bf16),
            dma((nk + nr,)),
            dma((nk, 6)),
            dma((nk, 6)),
            dma((tiles,)),
            dma((tiles,)),
            dma((nr, 6)),
            dma((nr, 6)),
        ],
        compiler_params=pltpu.CompilerParams(
            collective_id=0, has_side_effects=True, vmem_limit_bytes=56 * 1024 * 1024
        ),
        cost_estimate=pl.CostEstimate(
            flops=6 * total * hidden * width,
            bytes_accessed=2 * (gate_up.size + down.size),
            transcendentals=total * hidden,
        ),
    )(tokens, expert_ids.T, gate_weights.T, capacity, gate_up, down)


def expert_slots(expert_ids, gate_weights, capacity, expert, block_rows, slot_cap):
    total_rows = expert_ids.shape[0]
    member = expert_ids == expert
    hit_count = jnp.sum(member.astype(jnp.int32), axis=1)
    grouped = hit_count.reshape(total_rows // block_rows, block_rows)
    rank_in = (jnp.cumsum(grouped, axis=1) - grouped).reshape(total_rows)
    cap_here = lax.dynamic_index_in_dim(capacity, expert, 0, keepdims=False)
    usable = (hit_count > 0) & (rank_in < cap_here)
    weights = jnp.sum(jnp.where(member, gate_weights, 0.0), axis=1)
    groups = jnp.arange(total_rows, dtype=jnp.int32) // block_rows
    slot_ids = jnp.where(usable, groups * slot_cap + rank_in, -1)
    return (slot_ids, weights)


def local(tokens, gate_up, down, expert_ids, gate_weights, capacity):
    col_count = lax.axis_size("col")
    row_count = lax.axis_size("row")
    col_index = lax.axis_index("col")
    row_index = lax.axis_index("row")
    tok_dev = tokens.shape[0]
    block_rows = col_count * tok_dev
    slot_cap = min(3 * tok_dev * TOP // 2, block_rows)
    slot_count = row_count * slot_cap
    total_rows = expert_ids.shape[0]
    slot_ids, weights = expert_slots(
        expert_ids, gate_weights, capacity, col_index, block_rows, slot_cap
    )
    group_tokens = lax.all_gather(tokens, "col", axis=0, tiled=True)
    local_slots = (
        lax.dynamic_slice_in_dim(slot_ids, row_index * block_rows, block_rows)
        - row_index * slot_cap
    )
    cap_index = jnp.arange(slot_cap, dtype=jnp.int32)
    select = (cap_index[:, None] == local_slots[None, :]).astype(jnp.bfloat16)
    picked = jnp.dot(select, group_tokens, preferred_element_type=jnp.float32).astype(jnp.bfloat16)
    w_gate = gate_up[0, 0]
    w_up = gate_up[0, 1]
    contract = (((1,), (1,)), ((), ()))
    piece = lax.all_gather(picked, "row", axis=0, tiled=True)
    gate_part = lax.dot_general(piece, w_gate, contract, preferred_element_type=jnp.float32)
    up_part = lax.dot_general(piece, w_up, contract, preferred_element_type=jnp.float32)
    hidden = (jax.nn.silu(gate_part) * up_part).astype(jnp.bfloat16)
    w_down = down[0]
    outputs = jnp.dot(
        lax.all_gather(hidden, "row", axis=1, tiled=True),
        w_down,
        preferred_element_type=jnp.float32,
    ).astype(jnp.bfloat16)

    def by_column(values):
        return values.reshape(row_count, col_count, tok_dev).transpose(1, 0, 2).reshape(total_rows)

    column_slots = by_column(slot_ids)
    column_weights = by_column(weights)
    slot_index = jnp.arange(slot_count, dtype=jnp.int32)
    combine = jnp.where(
        column_slots[:, None] == slot_index[None, :], column_weights[:, None], 0.0
    ).astype(jnp.bfloat16)
    summed = lax.psum_scatter(
        jnp.dot(combine, outputs, preferred_element_type=jnp.float32),
        "col",
        scatter_dimension=0,
        tiled=True,
    )
    own_rows = lax.all_to_all(
        summed.astype(jnp.bfloat16), "row", split_axis=0, concat_axis=1, tiled=True
    ).astype(summed.dtype)
    return own_rows.astype(jnp.bfloat16)


def solution(mesh):
    in_specs = (
        P(("row", "col"), None),
        P("col", None, "row", None),
        P("col", None, "row"),
        P(),
        P(),
        P(),
    )
    out_specs = P(("row", "col"), None)
    small = mesh.shape["row"] == ROWS and mesh.shape["col"] == CORES * YS * ZS
    return jax.shard_map(
        fused if small else local, mesh=mesh, in_specs=in_specs, out_specs=out_specs, check_vma=False
    )
```

```python
import functools

import jax
import jax.numpy as jnp
from jax import lax
from jax.experimental import pallas as pl
from jax.experimental.pallas import tpu as pltpu
from jax.sharding import PartitionSpec as P

TOP = 8
MESH = pl.DeviceIdType.MESH
CORES, YS, ZS, ROWS = 2, 2, 4, 2
ORDERS = ("xzyc", "zxyc", "yzxc", "zyxc")
TILE = 256


def fused_kernel(
    nk,
    nr,
    tokens_ref,
    ids_ref,
    weights_ref,
    capacity_ref,
    gate_up_ref,
    down_ref,
    out_ref,
    wgu,
    wd,
    xbuf,
    x2d,
    acc,
    hid,
    yacc,
    zf,
    r1_out,
    r1_in,
    p1,
    r2_out,
    r2_in,
    p2,
    r3_out,
    r3_in,
    p3,
    r4_in,
    load_sem,
    g_send,
    g_recv,
    h_send,
    h_recv,
    r_send,
    r_recv,
):
    row = lax.axis_index("row")
    col = lax.axis_index("col")
    core = col % CORES
    y = (col // CORES) % YS
    z = col // (CORES * YS)
    tok_dev, width = tokens_ref.shape
    kc = width // nk
    tokens = x2d.shape[1]
    half = down_ref.shape[2]
    nc = half // nr
    hidden = gate_up_ref.shape[2]
    tiles = hidden // TILE

    x_peer = (1 - row, col)
    y_peer = (row, z * 4 + (1 - y) * 2 + core)
    core_peer = (row, z * 4 + y * 2 + 1 - core)
    z_places = (z + 1 - 2 * (z % 2), (z + 2) % ZS, ZS - 1 - z)
    z_peers = [(row, place * 4 + y * 2 + core) for place in z_places]

    def load_gu(k):
        columns = pl.ds(k * kc, kc)
        return pltpu.make_async_copy(
            gate_up_ref.at[0, :, :, columns], wgu.at[:, :, columns], load_sem.at[k]
        )

    def load_d(n):
        columns = pl.ds(n * nc, nc)
        return pltpu.make_async_copy(
            down_ref.at[0, :, columns], wd.at[:, columns], load_sem.at[nk + n]
        )

    for k in range(nk):
        load_gu(k).start()
    for n in range(nr):
        load_d(n).start()

    barrier = pltpu.get_barrier_semaphore()
    for peer in [x_peer, y_peer, core_peer] + z_peers:
        pl.semaphore_signal(barrier, inc=1, device_id=peer, device_id_type=MESH)
    for k in range(nk):
        xbuf[k, core, y, z, row] = tokens_ref[:, k * kc : (k + 1) * kc]
    pl.semaphore_wait(barrier, 6)

    def remote(src, dst, send, recv, peer):
        return pltpu.make_async_remote_copy(
            src_ref=src,
            dst_ref=dst,
            send_sem=send,
            recv_sem=recv,
            device_id=peer,
            device_id_type=MESH,
        )

    peers = {"x": [x_peer], "z": z_peers, "y": [y_peer], "c": [core_peer]}
    first_sem = {"x": 0, "z": 1, "y": 4, "c": 5}

    def gather(k, stage):
        order = ORDERS[k % len(ORDERS)]
        done, axis = order[:stage], order[stage]
        part = xbuf.at[
            k,
            core,
            slice(None) if "y" in done else y,
            slice(None) if "z" in done else z,
            slice(None) if "x" in done else row,
        ]
        return [
            remote(part, part, g_send.at[k, first_sem[axis] + i], g_recv.at[k, first_sem[axis] + i], peer)
            for i, peer in enumerate(peers[axis])
        ]

    started = []

    def start(copies):
        for copy in copies:
            copy.start()
            started.append(copy)

    def arrived(copies):
        for copy in copies:
            copy.wait_recv()

    def pass_on(k, stage):
        arrived(gather(k, stage - 1))
        start(gather(k, stage))

    for k in range(nk):
        start(gather(k, 0))
    for k in range(nk):
        pass_on(k, 1)

    member = ids_ref[...] == col
    hit_row = jnp.sum(member.astype(jnp.float32), axis=0, keepdims=True)
    weight_row = jnp.sum(jnp.where(member, weights_ref[...], 0.0), axis=0, keepdims=True)
    place = lax.broadcasted_iota(jnp.int32, (tokens, tokens), 0)
    other = lax.broadcasted_iota(jnp.int32, (tokens, tokens), 1)
    group = tokens // ROWS
    token = (
        ((place // 4) % 2) * group
        + ((place // 8) % 4) * 16
        + ((place // 32) % 2) * 8
        + (place // 64) * 4
        + place % 4
    )
    earlier = (other < token) & (other // group == token // group)
    rank = jnp.sum(jnp.where(earlier, hit_row, 0.0), axis=1, keepdims=True)
    same = other == token
    hit = jnp.sum(jnp.where(same, hit_row, 0.0), axis=1, keepdims=True)
    weight = jnp.sum(jnp.where(same, weight_row, 0.0), axis=1, keepdims=True)
    limit = capacity_ref[col].astype(jnp.float32)
    combine = jnp.where((hit > 0.5) & (rank < limit), weight, 0.0)
    combine = combine.astype(jnp.bfloat16).astype(jnp.float32)

    def send_hidden(h):
        part = hid.at[row, h]
        return [remote(part, part, h_send.at[h], h_recv.at[h], x_peer)]

    def product(k, part, first, count):
        return lax.dot_general(
            wgu[part, first : first + count, k * kc : (k + 1) * kc],
            x2d[k],
            (((1,), (1,)), ((), ())),
            preferred_element_type=jnp.float32,
        )

    for step in range(nk + 2):
        if step < nk:
            pass_on(step, 2)
        if 1 <= step <= nk:
            pass_on(step - 1, 3)
        if step < 2:
            continue
        k = step - 2
        arrived(gather(k, 3))
        block = xbuf[k].reshape(tokens // tok_dev, tok_dev, kc).astype(jnp.float32)
        x2d[k] = block.reshape(tokens, kc).astype(jnp.bfloat16)
        load_gu(k).wait()
        if k < nk - 1:
            for part in range(2):
                term = product(k, part, 0, hidden)
                acc[part] = term if k == 0 else acc[part] + term
            continue
        for h in range(tiles):
            rows = slice(h * TILE, (h + 1) * TILE)
            gate = acc[0, rows] + product(k, 0, h * TILE, TILE)
            up = acc[1, rows] + product(k, 1, h * TILE, TILE)
            act = gate / (1.0 + jnp.exp(-gate)) * up
            hid[row, h] = act.T.astype(jnp.bfloat16)
            start(send_hidden(h))

    def down_part(n, side):
        total = None
        for h in range(tiles):
            rows = pl.ds(pl.multiple_of(side * hidden + h * TILE, TILE), TILE)
            term = jnp.dot(
                hid[side, h],
                wd[rows, n * nc : (n + 1) * nc],
                preferred_element_type=jnp.float32,
            )
            total = term if total is None else total + term
        return total

    def reduce_1(n):
        return [remote(r1_out.at[n], r1_in.at[n], r_send.at[n, 0], r_recv.at[n, 0], core_peer)]

    def reduce_2(n):
        return [remote(r2_out.at[n], r2_in.at[n], r_send.at[n, 1], r_recv.at[n, 1], y_peer)]

    def reduce_3(n):
        return [
            remote(
                r3_out.at[n, z_places[i]],
                r3_in.at[n, i],
                r_send.at[n, 2 + i],
                r_recv.at[n, 2 + i],
                z_peers[i],
            )
            for i in range(ZS - 1)
        ]

    def reduce_4(n):
        return [
            remote(p3.at[n, 1 - row], r4_in.at[n], r_send.at[n, 5], r_recv.at[n, 5], x_peer)
        ]

    def after_core(n):
        arrived(reduce_1(n))
        both = zf[n, core] + r1_in[n].astype(jnp.float32)
        p1[n] = both.reshape(p1.shape[1:])
        r2_out[n] = p1[n, 1 - y].astype(jnp.bfloat16)
        start(reduce_2(n))

    def after_y(n):
        arrived(reduce_2(n))
        both = p1[n, y] + r2_in[n].astype(jnp.float32)
        p2[n] = both.reshape(p2.shape[1:])
        r3_out[n] = p2[n].astype(jnp.bfloat16)
        start(reduce_3(n))

    def after_z(n):
        arrived(reduce_3(n))
        total = p2[n, z]
        for i in range(ZS - 1):
            total = total + r3_in[n, i].astype(jnp.float32)
        p3[n, 0] = total[:tok_dev].astype(jnp.bfloat16)
        p3[n, 1] = total[tok_dev:].astype(jnp.bfloat16)
        start(reduce_4(n))

    for n in range(nr):
        load_d(n).wait()
        yacc[n] = down_part(n, row)
    for h in range(tiles):
        arrived(send_hidden(h))
    for n in range(nr + 3):
        if n < nr:
            total = (yacc[n] + down_part(n, 1 - row)).astype(jnp.bfloat16)
            scaled = total.astype(jnp.float32) * combine
            zf[n] = scaled.reshape(zf.shape[1:])
            r1_out[n] = zf[n, 1 - core].astype(jnp.bfloat16)
            start(reduce_1(n))
        if 1 <= n <= nr:
            after_core(n - 1)
        if 2 <= n <= nr + 1:
            after_y(n - 2)
        if n >= 3:
            after_z(n - 3)
    for n in range(nr):
        mine = pl.ds(pl.multiple_of(row * half + n * nc, 128), nc)
        theirs = pl.ds(pl.multiple_of((1 - row) * half + n * nc, 128), nc)
        out_ref[:, mine] = p3[n, row]
        arrived(reduce_4(n))
        out_ref[:, theirs] = r4_in[n]
    for copy in started:
        copy.wait_send()


def fused(tokens, gate_up, down, expert_ids, gate_weights, capacity):
    nk, nr = 4, 4
    tok_dev, width = tokens.shape
    total = expert_ids.shape[0]
    hidden = gate_up.shape[2]
    half = down.shape[2]
    kc, nc = width // nk, half // nr
    tiles = hidden // TILE
    vmem = pl.BlockSpec(memory_space=pltpu.VMEM)
    hbm = pl.BlockSpec(memory_space=pl.ANY)
    bf16, f32 = jnp.bfloat16, jnp.float32
    per_core, per_y, per_z = total // CORES, total // (CORES * YS), total // (CORES * YS * ZS)
    dma = pltpu.SemaphoreType.DMA
    return pl.pallas_call(
        functools.partial(fused_kernel, nk, nr),
        out_shape=jax.ShapeDtypeStruct(tokens.shape, bf16),
        in_specs=[vmem, vmem, vmem, pl.BlockSpec(memory_space=pltpu.SMEM), hbm, hbm],
        out_specs=vmem,
        scratch_shapes=[
            pltpu.VMEM((2, hidden, width), bf16),
            pltpu.VMEM((ROWS * hidden, half), bf16),
            pltpu.VMEM((nk, CORES, YS, ZS, ROWS, tok_dev, kc), bf16),
            pltpu.VMEM((nk, total, kc), bf16),
            pltpu.VMEM((2, hidden, total), f32),
            pltpu.VMEM((ROWS, tiles, total, TILE), bf16),
            pltpu.VMEM((nr, total, nc), f32),
            pltpu.VMEM((nr, CORES, per_core, nc), f32),
            pltpu.VMEM((nr, per_core, nc), bf16),
            pltpu.VMEM((nr, per_core, nc), bf16),
            pltpu.VMEM((nr, YS, per_y, nc), f32),
            pltpu.VMEM((nr, per_y, nc), bf16),
            pltpu.VMEM((nr, per_y, nc), bf16),
            pltpu.VMEM((nr, ZS, per_z, nc), f32),
            pltpu.VMEM((nr, ZS, per_z, nc), bf16),
            pltpu.VMEM((nr, ZS - 1, per_z, nc), bf16),
            pltpu.VMEM((nr, ROWS, tok_dev, nc), bf16),
            pltpu.VMEM((nr, tok_dev, nc), bf16),
            dma((nk + nr,)),
            dma((nk, 6)),
            dma((nk, 6)),
            dma((tiles,)),
            dma((tiles,)),
            dma((nr, 6)),
            dma((nr, 6)),
        ],
        compiler_params=pltpu.CompilerParams(
            collective_id=0, has_side_effects=True, vmem_limit_bytes=56 * 1024 * 1024
        ),
        cost_estimate=pl.CostEstimate(
            flops=6 * total * hidden * width,
            bytes_accessed=2 * (gate_up.size + down.size),
            transcendentals=total * hidden,
        ),
    )(tokens, expert_ids.T, gate_weights.T, capacity, gate_up, down)


def expert_slots(expert_ids, gate_weights, capacity, expert, block_rows, slot_cap):
    total_rows = expert_ids.shape[0]
    member = expert_ids == expert
    hit_count = jnp.sum(member.astype(jnp.int32), axis=1)
    grouped = hit_count.reshape(total_rows // block_rows, block_rows)
    rank_in = (jnp.cumsum(grouped, axis=1) - grouped).reshape(total_rows)
    cap_here = lax.dynamic_index_in_dim(capacity, expert, 0, keepdims=False)
    usable = (hit_count > 0) & (rank_in < cap_here)
    weights = jnp.sum(jnp.where(member, gate_weights, 0.0), axis=1)
    groups = jnp.arange(total_rows, dtype=jnp.int32) // block_rows
    slot_ids = jnp.where(usable, groups * slot_cap + rank_in, -1)
    return (slot_ids, weights)


def local(tokens, gate_up, down, expert_ids, gate_weights, capacity):
    col_count = lax.axis_size("col")
    row_count = lax.axis_size("row")
    col_index = lax.axis_index("col")
    row_index = lax.axis_index("row")
    tok_dev = tokens.shape[0]
    block_rows = col_count * tok_dev
    slot_cap = min(3 * tok_dev * TOP // 2, block_rows)
    slot_count = row_count * slot_cap
    total_rows = expert_ids.shape[0]
    slot_ids, weights = expert_slots(
        expert_ids, gate_weights, capacity, col_index, block_rows, slot_cap
    )
    group_tokens = lax.all_gather(tokens, "col", axis=0, tiled=True)
    local_slots = (
        lax.dynamic_slice_in_dim(slot_ids, row_index * block_rows, block_rows)
        - row_index * slot_cap
    )
    cap_index = jnp.arange(slot_cap, dtype=jnp.int32)
    select = (cap_index[:, None] == local_slots[None, :]).astype(jnp.bfloat16)
    picked = jnp.dot(select, group_tokens, preferred_element_type=jnp.float32).astype(jnp.bfloat16)
    w_gate = gate_up[0, 0]
    w_up = gate_up[0, 1]
    contract = (((1,), (1,)), ((), ()))
    piece = lax.all_gather(picked, "row", axis=0, tiled=True)
    gate_part = lax.dot_general(piece, w_gate, contract, preferred_element_type=jnp.float32)
    up_part = lax.dot_general(piece, w_up, contract, preferred_element_type=jnp.float32)
    hidden = (jax.nn.silu(gate_part) * up_part).astype(jnp.bfloat16)
    w_down = down[0]
    outputs = jnp.dot(
        lax.all_gather(hidden, "row", axis=1, tiled=True),
        w_down,
        preferred_element_type=jnp.float32,
    ).astype(jnp.bfloat16)

    def by_column(values):
        return values.reshape(row_count, col_count, tok_dev).transpose(1, 0, 2).reshape(total_rows)

    column_slots = by_column(slot_ids)
    column_weights = by_column(weights)
    slot_index = jnp.arange(slot_count, dtype=jnp.int32)
    combine = jnp.where(
        column_slots[:, None] == slot_index[None, :], column_weights[:, None], 0.0
    ).astype(jnp.bfloat16)
    summed = lax.psum_scatter(
        jnp.dot(combine, outputs, preferred_element_type=jnp.float32),
        "col",
        scatter_dimension=0,
        tiled=True,
    )
    own_rows = lax.all_to_all(
        summed.astype(jnp.bfloat16), "row", split_axis=0, concat_axis=1, tiled=True
    ).astype(summed.dtype)
    return own_rows.astype(jnp.bfloat16)


def solution(mesh):
    in_specs = (
        P(("row", "col"), None),
        P("col", None, "row", None),
        P("col", None, "row"),
        P(),
        P(),
        P(),
    )
    out_specs = P(("row", "col"), None)
    small = mesh.shape["row"] == ROWS and mesh.shape["col"] == CORES * YS * ZS
    return jax.shard_map(
        fused if small else local, mesh=mesh, in_specs=in_specs, out_specs=out_specs, check_vma=False
    )
```

```python
import functools

import jax
import jax.numpy as jnp
from jax import lax
from jax.experimental import pallas as pl
from jax.experimental.pallas import tpu as pltpu
from jax.sharding import PartitionSpec as P

TOP = 8
MESH = pl.DeviceIdType.MESH
CORES, YS, ZS, ROWS = 2, 2, 4, 2
ORDERS = ("xzyc", "zxyc", "yzxc", "zyxc")
TILE = 256


def fused_kernel(
    nk,
    nr,
    tokens_ref,
    ids_ref,
    weights_ref,
    capacity_ref,
    gate_up_ref,
    down_ref,
    out_ref,
    wgu,
    wd,
    xbuf,
    x2d,
    acc,
    hid,
    yacc,
    zf,
    r1_out,
    r1_in,
    p1,
    r2_out,
    r2_in,
    p2,
    r3_out,
    r3_in,
    p3,
    r4_in,
    load_sem,
    g_send,
    g_recv,
    h_send,
    h_recv,
    r_send,
    r_recv,
):
    row = lax.axis_index("row")
    col = lax.axis_index("col")
    core = col % CORES
    y = (col // CORES) % YS
    z = col // (CORES * YS)
    tok_dev, width = tokens_ref.shape
    kc = width // nk
    tokens = x2d.shape[1]
    half = down_ref.shape[2]
    nc = half // nr
    hidden = gate_up_ref.shape[2]
    tiles = hidden // TILE

    x_peer = (1 - row, col)
    y_peer = (row, z * 4 + (1 - y) * 2 + core)
    core_peer = (row, z * 4 + y * 2 + 1 - core)
    z_places = (z + 1 - 2 * (z % 2), (z + 2) % ZS, ZS - 1 - z)
    z_peers = [(row, place * 4 + y * 2 + core) for place in z_places]

    def load_gu(k):
        columns = pl.ds(k * kc, kc)
        return pltpu.make_async_copy(
            gate_up_ref.at[0, :, :, columns], wgu.at[:, :, columns], load_sem.at[k]
        )

    def load_d(n):
        columns = pl.ds(n * nc, nc)
        return pltpu.make_async_copy(
            down_ref.at[0, :, columns], wd.at[:, columns], load_sem.at[nk + n]
        )

    def start_gu(k):
        columns = pl.ds(k * kc, kc)
        for part in range(2):
            for h in range(tiles):
                rows = pl.ds(h * TILE, TILE)
                pltpu.make_async_copy(
                    gate_up_ref.at[0, part, rows, columns],
                    wgu.at[part, rows, columns],
                    load_sem.at[k],
                ).start(priority=1)

    def start_d(n):
        columns = pl.ds(n * nc, nc)
        for h in range(ROWS * tiles):
            rows = pl.ds(h * TILE, TILE)
            pltpu.make_async_copy(
                down_ref.at[0, rows, columns], wd.at[rows, columns], load_sem.at[nk + n]
            ).start(priority=1)

    start_gu(0)
    start_gu(1)

    barrier = pltpu.get_barrier_semaphore()
    for peer in [x_peer, y_peer, core_peer] + z_peers:
        pl.semaphore_signal(barrier, inc=1, device_id=peer, device_id_type=MESH)
    for k in range(nk):
        xbuf[k, core, y, z, row] = tokens_ref[:, k * kc : (k + 1) * kc]
    pl.semaphore_wait(barrier, 6)

    def remote(src, dst, send, recv, peer):
        return pltpu.make_async_remote_copy(
            src_ref=src,
            dst_ref=dst,
            send_sem=send,
            recv_sem=recv,
            device_id=peer,
            device_id_type=MESH,
        )

    peers = {"x": [x_peer], "z": z_peers, "y": [y_peer], "c": [core_peer]}
    first_sem = {"x": 0, "z": 1, "y": 4, "c": 5}

    def gather(k, stage):
        order = ORDERS[k % len(ORDERS)]
        done, axis = order[:stage], order[stage]
        part = xbuf.at[
            k,
            core,
            slice(None) if "y" in done else y,
            slice(None) if "z" in done else z,
            slice(None) if "x" in done else row,
        ]
        return [
            remote(part, part, g_send.at[k, first_sem[axis] + i], g_recv.at[k, first_sem[axis] + i], peer)
            for i, peer in enumerate(peers[axis])
        ]

    started = []

    def start(copies):
        for copy in copies:
            copy.start()
            started.append(copy)

    def arrived(copies):
        for copy in copies:
            copy.wait_recv()

    def pass_on(k, stage):
        arrived(gather(k, stage - 1))
        start(gather(k, stage))

    for k in range(nk):
        start(gather(k, 0))
    for k in range(nk):
        pass_on(k, 1)
    start_gu(2)

    member = ids_ref[...] == col
    hit_row = jnp.sum(member.astype(jnp.float32), axis=0, keepdims=True)
    weight_row = jnp.sum(jnp.where(member, weights_ref[...], 0.0), axis=0, keepdims=True)
    place = lax.broadcasted_iota(jnp.int32, (tokens, tokens), 0)
    other = lax.broadcasted_iota(jnp.int32, (tokens, tokens), 1)
    group = tokens // ROWS
    token = (
        ((place // 4) % 2) * group
        + ((place // 8) % 4) * 16
        + ((place // 32) % 2) * 8
        + (place // 64) * 4
        + place % 4
    )
    earlier = (other < token) & (other // group == token // group)
    rank = jnp.sum(jnp.where(earlier, hit_row, 0.0), axis=1, keepdims=True)
    same = other == token
    hit = jnp.sum(jnp.where(same, hit_row, 0.0), axis=1, keepdims=True)
    weight = jnp.sum(jnp.where(same, weight_row, 0.0), axis=1, keepdims=True)
    limit = capacity_ref[col].astype(jnp.float32)
    combine = jnp.where((hit > 0.5) & (rank < limit), weight, 0.0)
    combine = combine.astype(jnp.bfloat16).astype(jnp.float32)

    def send_hidden(h):
        part = hid.at[row, h]
        return [remote(part, part, h_send.at[h], h_recv.at[h], x_peer)]

    def product(k, part, first, count):
        return lax.dot_general(
            wgu[part, first : first + count, k * kc : (k + 1) * kc],
            x2d[k],
            (((1,), (1,)), ((), ())),
            preferred_element_type=jnp.float32,
        )

    for step in range(nk + 2):
        if step < nk:
            pass_on(step, 2)
        if step == 1:
            for k in range(3, nk):
                start_gu(k)
        if 2 <= step < 4:
            for n in range(step - 2, nr, 2):
                start_d(n)
        if 1 <= step <= nk:
            pass_on(step - 1, 3)
        if step < 2:
            continue
        k = step - 2
        arrived(gather(k, 3))
        block = xbuf[k].reshape(tokens // tok_dev, tok_dev, kc).astype(jnp.float32)
        x2d[k] = block.reshape(tokens, kc).astype(jnp.bfloat16)
        load_gu(k).wait()
        if k < nk - 1:
            for part in range(2):
                term = product(k, part, 0, hidden)
                acc[part] = term if k == 0 else acc[part] + term
            continue
        for h in range(tiles):
            rows = slice(h * TILE, (h + 1) * TILE)
            gate = acc[0, rows] + product(k, 0, h * TILE, TILE)
            up = acc[1, rows] + product(k, 1, h * TILE, TILE)
            act = gate / (1.0 + jnp.exp(-gate)) * up
            hid[row, h] = act.T.astype(jnp.bfloat16)
            start(send_hidden(h))

    def down_part(n, side):
        total = None
        for h in range(tiles):
            rows = pl.ds(pl.multiple_of(side * hidden + h * TILE, TILE), TILE)
            term = jnp.dot(
                hid[side, h],
                wd[rows, n * nc : (n + 1) * nc],
                preferred_element_type=jnp.float32,
            )
            total = term if total is None else total + term
        return total

    def reduce_1(n):
        return [remote(r1_out.at[n], r1_in.at[n], r_send.at[n, 0], r_recv.at[n, 0], core_peer)]

    def reduce_2(n):
        return [remote(r2_out.at[n], r2_in.at[n], r_send.at[n, 1], r_recv.at[n, 1], y_peer)]

    def reduce_3(n):
        return [
            remote(
                r3_out.at[n, z_places[i]],
                r3_in.at[n, i],
                r_send.at[n, 2 + i],
                r_recv.at[n, 2 + i],
                z_peers[i],
            )
            for i in range(ZS - 1)
        ]

    def reduce_4(n):
        return [
            remote(p3.at[n, 1 - row], r4_in.at[n], r_send.at[n, 5], r_recv.at[n, 5], x_peer)
        ]

    def after_core(n):
        arrived(reduce_1(n))
        both = zf[n, core] + r1_in[n].astype(jnp.float32)
        p1[n] = both.reshape(p1.shape[1:])
        r2_out[n] = p1[n, 1 - y].astype(jnp.bfloat16)
        start(reduce_2(n))

    def after_y(n):
        arrived(reduce_2(n))
        both = p1[n, y] + r2_in[n].astype(jnp.float32)
        p2[n] = both.reshape(p2.shape[1:])
        r3_out[n] = p2[n].astype(jnp.bfloat16)
        start(reduce_3(n))

    def after_z(n):
        arrived(reduce_3(n))
        total = p2[n, z]
        for i in range(ZS - 1):
            total = total + r3_in[n, i].astype(jnp.float32)
        p3[n, 0] = total[:tok_dev].astype(jnp.bfloat16)
        p3[n, 1] = total[tok_dev:].astype(jnp.bfloat16)
        start(reduce_4(n))

    for n in range(nr):
        load_d(n).wait()
        yacc[n] = down_part(n, row)
    for h in range(tiles):
        arrived(send_hidden(h))
    for n in range(nr + 3):
        if n < nr:
            total = (yacc[n] + down_part(n, 1 - row)).astype(jnp.bfloat16)
            scaled = total.astype(jnp.float32) * combine
            zf[n] = scaled.reshape(zf.shape[1:])
            r1_out[n] = zf[n, 1 - core].astype(jnp.bfloat16)
            start(reduce_1(n))
        if 1 <= n <= nr:
            after_core(n - 1)
        if 2 <= n <= nr + 1:
            after_y(n - 2)
        if n >= 3:
            after_z(n - 3)
    for n in range(nr):
        mine = pl.ds(pl.multiple_of(row * half + n * nc, 128), nc)
        theirs = pl.ds(pl.multiple_of((1 - row) * half + n * nc, 128), nc)
        out_ref[:, mine] = p3[n, row]
        arrived(reduce_4(n))
        out_ref[:, theirs] = r4_in[n]
    for copy in started:
        copy.wait_send()


def fused(tokens, gate_up, down, expert_ids, gate_weights, capacity):
    nk, nr = 4, 4
    tok_dev, width = tokens.shape
    total = expert_ids.shape[0]
    hidden = gate_up.shape[2]
    half = down.shape[2]
    kc, nc = width // nk, half // nr
    tiles = hidden // TILE
    vmem = pl.BlockSpec(memory_space=pltpu.VMEM)
    hbm = pl.BlockSpec(memory_space=pl.ANY)
    bf16, f32 = jnp.bfloat16, jnp.float32
    per_core, per_y, per_z = total // CORES, total // (CORES * YS), total // (CORES * YS * ZS)
    dma = pltpu.SemaphoreType.DMA
    return pl.pallas_call(
        functools.partial(fused_kernel, nk, nr),
        out_shape=jax.ShapeDtypeStruct(tokens.shape, bf16),
        in_specs=[vmem, vmem, vmem, pl.BlockSpec(memory_space=pltpu.SMEM), hbm, hbm],
        out_specs=vmem,
        scratch_shapes=[
            pltpu.VMEM((2, hidden, width), bf16),
            pltpu.VMEM((ROWS * hidden, half), bf16),
            pltpu.VMEM((nk, CORES, YS, ZS, ROWS, tok_dev, kc), bf16),
            pltpu.VMEM((nk, total, kc), bf16),
            pltpu.VMEM((2, hidden, total), f32),
            pltpu.VMEM((ROWS, tiles, total, TILE), bf16),
            pltpu.VMEM((nr, total, nc), f32),
            pltpu.VMEM((nr, CORES, per_core, nc), f32),
            pltpu.VMEM((nr, per_core, nc), bf16),
            pltpu.VMEM((nr, per_core, nc), bf16),
            pltpu.VMEM((nr, YS, per_y, nc), f32),
            pltpu.VMEM((nr, per_y, nc), bf16),
            pltpu.VMEM((nr, per_y, nc), bf16),
            pltpu.VMEM((nr, ZS, per_z, nc), f32),
            pltpu.VMEM((nr, ZS, per_z, nc), bf16),
            pltpu.VMEM((nr, ZS - 1, per_z, nc), bf16),
            pltpu.VMEM((nr, ROWS, tok_dev, nc), bf16),
            pltpu.VMEM((nr, tok_dev, nc), bf16),
            dma((nk + nr,)),
            dma((nk, 6)),
            dma((nk, 6)),
            dma((tiles,)),
            dma((tiles,)),
            dma((nr, 6)),
            dma((nr, 6)),
        ],
        compiler_params=pltpu.CompilerParams(
            collective_id=0, has_side_effects=True, vmem_limit_bytes=56 * 1024 * 1024
        ),
        cost_estimate=pl.CostEstimate(
            flops=6 * total * hidden * width,
            bytes_accessed=2 * (gate_up.size + down.size),
            transcendentals=total * hidden,
        ),
    )(tokens, expert_ids.T, gate_weights.T, capacity, gate_up, down)


def expert_slots(expert_ids, gate_weights, capacity, expert, block_rows, slot_cap):
    total_rows = expert_ids.shape[0]
    member = expert_ids == expert
    hit_count = jnp.sum(member.astype(jnp.int32), axis=1)
    grouped = hit_count.reshape(total_rows // block_rows, block_rows)
    rank_in = (jnp.cumsum(grouped, axis=1) - grouped).reshape(total_rows)
    cap_here = lax.dynamic_index_in_dim(capacity, expert, 0, keepdims=False)
    usable = (hit_count > 0) & (rank_in < cap_here)
    weights = jnp.sum(jnp.where(member, gate_weights, 0.0), axis=1)
    groups = jnp.arange(total_rows, dtype=jnp.int32) // block_rows
    slot_ids = jnp.where(usable, groups * slot_cap + rank_in, -1)
    return (slot_ids, weights)


def local(tokens, gate_up, down, expert_ids, gate_weights, capacity):
    col_count = lax.axis_size("col")
    row_count = lax.axis_size("row")
    col_index = lax.axis_index("col")
    row_index = lax.axis_index("row")
    tok_dev = tokens.shape[0]
    block_rows = col_count * tok_dev
    slot_cap = min(3 * tok_dev * TOP // 2, block_rows)
    slot_count = row_count * slot_cap
    total_rows = expert_ids.shape[0]
    slot_ids, weights = expert_slots(
        expert_ids, gate_weights, capacity, col_index, block_rows, slot_cap
    )
    group_tokens = lax.all_gather(tokens, "col", axis=0, tiled=True)
    local_slots = (
        lax.dynamic_slice_in_dim(slot_ids, row_index * block_rows, block_rows)
        - row_index * slot_cap
    )
    cap_index = jnp.arange(slot_cap, dtype=jnp.int32)
    select = (cap_index[:, None] == local_slots[None, :]).astype(jnp.bfloat16)
    picked = jnp.dot(select, group_tokens, preferred_element_type=jnp.float32).astype(jnp.bfloat16)
    w_gate = gate_up[0, 0]
    w_up = gate_up[0, 1]
    contract = (((1,), (1,)), ((), ()))
    piece = lax.all_gather(picked, "row", axis=0, tiled=True)
    gate_part = lax.dot_general(piece, w_gate, contract, preferred_element_type=jnp.float32)
    up_part = lax.dot_general(piece, w_up, contract, preferred_element_type=jnp.float32)
    hidden = (jax.nn.silu(gate_part) * up_part).astype(jnp.bfloat16)
    w_down = down[0]
    outputs = jnp.dot(
        lax.all_gather(hidden, "row", axis=1, tiled=True),
        w_down,
        preferred_element_type=jnp.float32,
    ).astype(jnp.bfloat16)

    def by_column(values):
        return values.reshape(row_count, col_count, tok_dev).transpose(1, 0, 2).reshape(total_rows)

    column_slots = by_column(slot_ids)
    column_weights = by_column(weights)
    slot_index = jnp.arange(slot_count, dtype=jnp.int32)
    combine = jnp.where(
        column_slots[:, None] == slot_index[None, :], column_weights[:, None], 0.0
    ).astype(jnp.bfloat16)
    summed = lax.psum_scatter(
        jnp.dot(combine, outputs, preferred_element_type=jnp.float32),
        "col",
        scatter_dimension=0,
        tiled=True,
    )
    own_rows = lax.all_to_all(
        summed.astype(jnp.bfloat16), "row", split_axis=0, concat_axis=1, tiled=True
    ).astype(summed.dtype)
    return own_rows.astype(jnp.bfloat16)


def solution(mesh):
    in_specs = (
        P(("row", "col"), None),
        P("col", None, "row", None),
        P("col", None, "row"),
        P(),
        P(),
        P(),
    )
    out_specs = P(("row", "col"), None)
    small = mesh.shape["row"] == ROWS and mesh.shape["col"] == CORES * YS * ZS
    return jax.shard_map(
        fused if small else local, mesh=mesh, in_specs=in_specs, out_specs=out_specs, check_vma=False
    )
```

```python
import functools

import jax
import jax.numpy as jnp
from jax import lax
from jax.experimental import pallas as pl
from jax.experimental.pallas import tpu as pltpu
from jax.sharding import PartitionSpec as P

TOP = 8
MESH = pl.DeviceIdType.MESH
CORES, YS, ZS, ROWS = 2, 2, 4, 2
ORDERS = ("xzyc", "yzxc")
TILE = 256


def fused_kernel(
    nk,
    nr,
    tokens_ref,
    ids_ref,
    weights_ref,
    capacity_ref,
    gate_up_ref,
    down_ref,
    out_ref,
    wgu,
    wd,
    xbuf,
    x2d,
    acc,
    hid,
    yacc,
    zf,
    r1_out,
    r1_in,
    p1,
    r2_out,
    r2_in,
    p2,
    r3_out,
    r3_in,
    p3,
    r4_in,
    load_sem,
    g_send,
    g_recv,
    h_send,
    h_recv,
    r_send,
    r_recv,
):
    row = lax.axis_index("row")
    col = lax.axis_index("col")
    core = col % CORES
    y = (col // CORES) % YS
    z = col // (CORES * YS)
    tok_dev, width = tokens_ref.shape
    kc = width // nk
    tokens = x2d.shape[1]
    half = down_ref.shape[2]
    nc = half // nr
    hidden = gate_up_ref.shape[2]
    tiles = hidden // TILE

    x_peer = (1 - row, col)
    y_peer = (row, z * 4 + (1 - y) * 2 + core)
    core_peer = (row, z * 4 + y * 2 + 1 - core)
    z_places = (z + 1 - 2 * (z % 2), (z + 2) % ZS, ZS - 1 - z)
    z_peers = [(row, place * 4 + y * 2 + core) for place in z_places]

    def load_gu(k):
        columns = pl.ds(k * kc, kc)
        return pltpu.make_async_copy(
            gate_up_ref.at[0, :, :, columns], wgu.at[:, :, columns], load_sem.at[k]
        )

    def load_d(n):
        columns = pl.ds(n * nc, nc)
        return pltpu.make_async_copy(
            down_ref.at[0, :, columns], wd.at[:, columns], load_sem.at[nk + n]
        )

    for k in range(nk):
        load_gu(k).start()
    for n in range(nr):
        load_d(n).start()

    barrier = pltpu.get_barrier_semaphore()
    for peer in [x_peer, y_peer, core_peer] + z_peers:
        pl.semaphore_signal(barrier, inc=1, device_id=peer, device_id_type=MESH)
    for k in range(nk):
        xbuf[k, core, y, z, row] = tokens_ref[:, k * kc : (k + 1) * kc]
    pl.semaphore_wait(barrier, 6)

    def remote(src, dst, send, recv, peer):
        return pltpu.make_async_remote_copy(
            src_ref=src,
            dst_ref=dst,
            send_sem=send,
            recv_sem=recv,
            device_id=peer,
            device_id_type=MESH,
        )

    peers = {"x": [x_peer], "z": z_peers, "y": [y_peer], "c": [core_peer]}
    first_sem = {"x": 0, "z": 1, "y": 4, "c": 5}

    def gather(k, stage):
        order = ORDERS[k % len(ORDERS)]
        done, axis = order[:stage], order[stage]
        part = xbuf.at[
            k,
            core,
            slice(None) if "y" in done else y,
            slice(None) if "z" in done else z,
            slice(None) if "x" in done else row,
        ]
        return [
            remote(part, part, g_send.at[k, first_sem[axis] + i], g_recv.at[k, first_sem[axis] + i], peer)
            for i, peer in enumerate(peers[axis])
        ]

    started = []

    def start(copies):
        for copy in copies:
            copy.start()
            started.append(copy)

    def arrived(copies):
        for copy in copies:
            copy.wait_recv()

    def pass_on(k, stage):
        arrived(gather(k, stage - 1))
        start(gather(k, stage))

    for k in range(nk):
        start(gather(k, 0))
    for k in range(nk):
        pass_on(k, 1)

    member = ids_ref[...] == col
    hit_row = jnp.sum(member.astype(jnp.float32), axis=0, keepdims=True)
    weight_row = jnp.sum(jnp.where(member, weights_ref[...], 0.0), axis=0, keepdims=True)
    place = lax.broadcasted_iota(jnp.int32, (tokens, tokens), 0)
    other = lax.broadcasted_iota(jnp.int32, (tokens, tokens), 1)
    group = tokens // ROWS
    token = (
        ((place // 4) % 2) * group
        + ((place // 8) % 4) * 16
        + ((place // 32) % 2) * 8
        + (place // 64) * 4
        + place % 4
    )
    earlier = (other < token) & (other // group == token // group)
    rank = jnp.sum(jnp.where(earlier, hit_row, 0.0), axis=1, keepdims=True)
    same = other == token
    hit = jnp.sum(jnp.where(same, hit_row, 0.0), axis=1, keepdims=True)
    weight = jnp.sum(jnp.where(same, weight_row, 0.0), axis=1, keepdims=True)
    limit = capacity_ref[col].astype(jnp.float32)
    combine = jnp.where((hit > 0.5) & (rank < limit), weight, 0.0)
    combine = combine.astype(jnp.bfloat16).astype(jnp.float32)

    def send_hidden(h):
        part = hid.at[row, h]
        return [remote(part, part, h_send.at[h], h_recv.at[h], x_peer)]

    def product(k, part, first, count):
        return lax.dot_general(
            wgu[part, first : first + count, k * kc : (k + 1) * kc],
            x2d[k],
            (((1,), (1,)), ((), ())),
            preferred_element_type=jnp.float32,
        )

    for step in range(nk + 2):
        if step < nk:
            pass_on(step, 2)
        if 1 <= step <= nk:
            pass_on(step - 1, 3)
        if step < 2:
            continue
        k = step - 2
        arrived(gather(k, 3))
        block = xbuf[k].reshape(tokens // tok_dev, tok_dev, kc).astype(jnp.float32)
        x2d[k] = block.reshape(tokens, kc).astype(jnp.bfloat16)
        load_gu(k).wait()
        if k < nk - 1:
            for part in range(2):
                term = product(k, part, 0, hidden)
                acc[part] = term if k == 0 else acc[part] + term
            continue
        for h in range(tiles):
            rows = slice(h * TILE, (h + 1) * TILE)
            gate = acc[0, rows] + product(k, 0, h * TILE, TILE)
            up = acc[1, rows] + product(k, 1, h * TILE, TILE)
            act = gate / (1.0 + jnp.exp(-gate)) * up
            hid[row, h] = act.T.astype(jnp.bfloat16)
            start(send_hidden(h))

    def down_part(n, side):
        total = None
        for h in range(tiles):
            rows = pl.ds(pl.multiple_of(side * hidden + h * TILE, TILE), TILE)
            term = jnp.dot(
                hid[side, h],
                wd[rows, n * nc : (n + 1) * nc],
                preferred_element_type=jnp.float32,
            )
            total = term if total is None else total + term
        return total

    def reduce_1(n):
        return [remote(r1_out.at[n], r1_in.at[n], r_send.at[n, 0], r_recv.at[n, 0], core_peer)]

    def reduce_2(n):
        return [remote(r2_out.at[n], r2_in.at[n], r_send.at[n, 1], r_recv.at[n, 1], y_peer)]

    def reduce_3(n):
        return [
            remote(
                r3_out.at[n, z_places[i]],
                r3_in.at[n, i],
                r_send.at[n, 2 + i],
                r_recv.at[n, 2 + i],
                z_peers[i],
            )
            for i in range(ZS - 1)
        ]

    def reduce_4(n):
        return [
            remote(p3.at[n, 1 - row], r4_in.at[n], r_send.at[n, 5], r_recv.at[n, 5], x_peer)
        ]

    def after_core(n):
        arrived(reduce_1(n))
        both = zf[n, core] + r1_in[n].astype(jnp.float32)
        p1[n] = both.reshape(p1.shape[1:])
        r2_out[n] = p1[n, 1 - y].astype(jnp.bfloat16)
        start(reduce_2(n))

    def after_y(n):
        arrived(reduce_2(n))
        both = p1[n, y] + r2_in[n].astype(jnp.float32)
        p2[n] = both.reshape(p2.shape[1:])
        r3_out[n] = p2[n].astype(jnp.bfloat16)
        start(reduce_3(n))

    def after_z(n):
        arrived(reduce_3(n))
        total = p2[n, z]
        for i in range(ZS - 1):
            total = total + r3_in[n, i].astype(jnp.float32)
        p3[n, 0] = total[:tok_dev].astype(jnp.bfloat16)
        p3[n, 1] = total[tok_dev:].astype(jnp.bfloat16)
        start(reduce_4(n))

    for n in range(nr):
        load_d(n).wait()
        yacc[n] = down_part(n, row)
    for h in range(tiles):
        arrived(send_hidden(h))
    for n in range(nr + 3):
        if n < nr:
            total = (yacc[n] + down_part(n, 1 - row)).astype(jnp.bfloat16)
            scaled = total.astype(jnp.float32) * combine
            zf[n] = scaled.reshape(zf.shape[1:])
            r1_out[n] = zf[n, 1 - core].astype(jnp.bfloat16)
            start(reduce_1(n))
        if 1 <= n <= nr:
            after_core(n - 1)
        if 2 <= n <= nr + 1:
            after_y(n - 2)
        if n >= 3:
            after_z(n - 3)
    for n in range(nr):
        mine = pl.ds(pl.multiple_of(row * half + n * nc, 128), nc)
        theirs = pl.ds(pl.multiple_of((1 - row) * half + n * nc, 128), nc)
        out_ref[:, mine] = p3[n, row]
        arrived(reduce_4(n))
        out_ref[:, theirs] = r4_in[n]
    for copy in started:
        copy.wait_send()


def fused(tokens, gate_up, down, expert_ids, gate_weights, capacity):
    nk, nr = 7, 7
    tok_dev, width = tokens.shape
    total = expert_ids.shape[0]
    hidden = gate_up.shape[2]
    half = down.shape[2]
    kc, nc = width // nk, half // nr
    tiles = hidden // TILE
    vmem = pl.BlockSpec(memory_space=pltpu.VMEM)
    hbm = pl.BlockSpec(memory_space=pl.ANY)
    bf16, f32 = jnp.bfloat16, jnp.float32
    per_core, per_y, per_z = total // CORES, total // (CORES * YS), total // (CORES * YS * ZS)
    dma = pltpu.SemaphoreType.DMA
    return pl.pallas_call(
        functools.partial(fused_kernel, nk, nr),
        out_shape=jax.ShapeDtypeStruct(tokens.shape, bf16),
        in_specs=[vmem, vmem, vmem, pl.BlockSpec(memory_space=pltpu.SMEM), hbm, hbm],
        out_specs=vmem,
        scratch_shapes=[
            pltpu.VMEM((2, hidden, width), bf16),
            pltpu.VMEM((ROWS * hidden, half), bf16),
            pltpu.VMEM((nk, CORES, YS, ZS, ROWS, tok_dev, kc), bf16),
            pltpu.VMEM((nk, total, kc), bf16),
            pltpu.VMEM((2, hidden, total), f32),
            pltpu.VMEM((ROWS, tiles, total, TILE), bf16),
            pltpu.VMEM((nr, total, nc), f32),
            pltpu.VMEM((nr, CORES, per_core, nc), f32),
            pltpu.VMEM((nr, per_core, nc), bf16),
            pltpu.VMEM((nr, per_core, nc), bf16),
            pltpu.VMEM((nr, YS, per_y, nc), f32),
            pltpu.VMEM((nr, per_y, nc), bf16),
            pltpu.VMEM((nr, per_y, nc), bf16),
            pltpu.VMEM((nr, ZS, per_z, nc), f32),
            pltpu.VMEM((nr, ZS, per_z, nc), bf16),
            pltpu.VMEM((nr, ZS - 1, per_z, nc), bf16),
            pltpu.VMEM((nr, ROWS, tok_dev, nc), bf16),
            pltpu.VMEM((nr, tok_dev, nc), bf16),
            dma((nk + nr,)),
            dma((nk, 6)),
            dma((nk, 6)),
            dma((tiles,)),
            dma((tiles,)),
            dma((nr, 6)),
            dma((nr, 6)),
        ],
        compiler_params=pltpu.CompilerParams(
            collective_id=0, has_side_effects=True, vmem_limit_bytes=56 * 1024 * 1024
        ),
        cost_estimate=pl.CostEstimate(
            flops=6 * total * hidden * width,
            bytes_accessed=2 * (gate_up.size + down.size),
            transcendentals=total * hidden,
        ),
    )(tokens, expert_ids.T, gate_weights.T, capacity, gate_up, down)


def expert_slots(expert_ids, gate_weights, capacity, expert, block_rows, slot_cap):
    total_rows = expert_ids.shape[0]
    member = expert_ids == expert
    hit_count = jnp.sum(member.astype(jnp.int32), axis=1)
    grouped = hit_count.reshape(total_rows // block_rows, block_rows)
    rank_in = (jnp.cumsum(grouped, axis=1) - grouped).reshape(total_rows)
    cap_here = lax.dynamic_index_in_dim(capacity, expert, 0, keepdims=False)
    usable = (hit_count > 0) & (rank_in < cap_here)
    weights = jnp.sum(jnp.where(member, gate_weights, 0.0), axis=1)
    groups = jnp.arange(total_rows, dtype=jnp.int32) // block_rows
    slot_ids = jnp.where(usable, groups * slot_cap + rank_in, -1)
    return (slot_ids, weights)


def local(tokens, gate_up, down, expert_ids, gate_weights, capacity):
    col_count = lax.axis_size("col")
    row_count = lax.axis_size("row")
    col_index = lax.axis_index("col")
    row_index = lax.axis_index("row")
    tok_dev = tokens.shape[0]
    block_rows = col_count * tok_dev
    slot_cap = min(3 * tok_dev * TOP // 2, block_rows)
    slot_count = row_count * slot_cap
    total_rows = expert_ids.shape[0]
    slot_ids, weights = expert_slots(
        expert_ids, gate_weights, capacity, col_index, block_rows, slot_cap
    )
    group_tokens = lax.all_gather(tokens, "col", axis=0, tiled=True)
    local_slots = (
        lax.dynamic_slice_in_dim(slot_ids, row_index * block_rows, block_rows)
        - row_index * slot_cap
    )
    cap_index = jnp.arange(slot_cap, dtype=jnp.int32)
    select = (cap_index[:, None] == local_slots[None, :]).astype(jnp.bfloat16)
    picked = jnp.dot(select, group_tokens, preferred_element_type=jnp.float32).astype(jnp.bfloat16)
    w_gate = gate_up[0, 0]
    w_up = gate_up[0, 1]
    contract = (((1,), (1,)), ((), ()))
    piece = lax.all_gather(picked, "row", axis=0, tiled=True)
    gate_part = lax.dot_general(piece, w_gate, contract, preferred_element_type=jnp.float32)
    up_part = lax.dot_general(piece, w_up, contract, preferred_element_type=jnp.float32)
    hidden = (jax.nn.silu(gate_part) * up_part).astype(jnp.bfloat16)
    w_down = down[0]
    outputs = jnp.dot(
        lax.all_gather(hidden, "row", axis=1, tiled=True),
        w_down,
        preferred_element_type=jnp.float32,
    ).astype(jnp.bfloat16)

    def by_column(values):
        return values.reshape(row_count, col_count, tok_dev).transpose(1, 0, 2).reshape(total_rows)

    column_slots = by_column(slot_ids)
    column_weights = by_column(weights)
    slot_index = jnp.arange(slot_count, dtype=jnp.int32)
    combine = jnp.where(
        column_slots[:, None] == slot_index[None, :], column_weights[:, None], 0.0
    ).astype(jnp.bfloat16)
    summed = lax.psum_scatter(
        jnp.dot(combine, outputs, preferred_element_type=jnp.float32),
        "col",
        scatter_dimension=0,
        tiled=True,
    )
    own_rows = lax.all_to_all(
        summed.astype(jnp.bfloat16), "row", split_axis=0, concat_axis=1, tiled=True
    ).astype(summed.dtype)
    return own_rows.astype(jnp.bfloat16)


def solution(mesh):
    in_specs = (
        P(("row", "col"), None),
        P("col", None, "row", None),
        P("col", None, "row"),
        P(),
        P(),
        P(),
    )
    out_specs = P(("row", "col"), None)
    small = mesh.shape["row"] == ROWS and mesh.shape["col"] == CORES * YS * ZS
    return jax.shard_map(
        fused if small else local, mesh=mesh, in_specs=in_specs, out_specs=out_specs, check_vma=False
    )
```

```python
import functools

import jax
import jax.numpy as jnp
from jax import lax
from jax.experimental import pallas as pl
from jax.experimental.pallas import tpu as pltpu
from jax.sharding import PartitionSpec as P

TOP = 8
MESH = pl.DeviceIdType.MESH
CORES, YS, ZS, ROWS = 2, 2, 4, 2
ORDERS = ("xzyc", "yzxc")
TILE = 256


def fused_kernel(
    nk,
    nr,
    tokens_ref,
    ids_ref,
    weights_ref,
    capacity_ref,
    gate_up_ref,
    down_ref,
    out_ref,
    wgu,
    wd,
    xbuf,
    x2d,
    acc,
    hid,
    yacc,
    zf,
    r1_out,
    r1_in,
    p1,
    r2_out,
    r2_in,
    p2,
    r3_out,
    r3_in,
    p3,
    r4_in,
    load_sem,
    g_send,
    g_recv,
    h_send,
    h_recv,
    r_send,
    r_recv,
):
    row = lax.axis_index("row")
    col = lax.axis_index("col")
    core = col % CORES
    y = (col // CORES) % YS
    z = col // (CORES * YS)
    tok_dev, width = tokens_ref.shape
    kc = width // nk
    tokens = x2d.shape[1]
    half = down_ref.shape[2]
    nc = half // nr
    hidden = gate_up_ref.shape[2]
    tiles = hidden // TILE

    x_peer = (1 - row, col)
    y_peer = (row, z * 4 + (1 - y) * 2 + core)
    core_peer = (row, z * 4 + y * 2 + 1 - core)
    z_places = (z + 1 - 2 * (z % 2), (z + 2) % ZS, ZS - 1 - z)
    z_peers = [(row, place * 4 + y * 2 + core) for place in z_places]

    def load_gu(k):
        columns = pl.ds(k * kc, kc)
        return pltpu.make_async_copy(
            gate_up_ref.at[0, :, :, columns], wgu.at[:, :, columns], load_sem.at[k]
        )

    def load_d(n):
        columns = pl.ds(n * nc, nc)
        return pltpu.make_async_copy(
            down_ref.at[0, :, columns], wd.at[:, columns], load_sem.at[nk + n]
        )

    for k in range(nk):
        load_gu(k).start()
    for n in range(nr):
        load_d(n).start()

    barrier = pltpu.get_barrier_semaphore()
    for peer in [x_peer, y_peer, core_peer] + z_peers:
        pl.semaphore_signal(barrier, inc=1, device_id=peer, device_id_type=MESH)
    for k in range(nk):
        xbuf[k, core, y, z, row] = tokens_ref[:, k * kc : (k + 1) * kc]
    pl.semaphore_wait(barrier, 6)

    def remote(src, dst, send, recv, peer):
        return pltpu.make_async_remote_copy(
            src_ref=src,
            dst_ref=dst,
            send_sem=send,
            recv_sem=recv,
            device_id=peer,
            device_id_type=MESH,
        )

    peers = {"x": [x_peer], "z": z_peers, "y": [y_peer], "c": [core_peer]}
    first_sem = {"x": 0, "z": 1, "y": 4, "c": 5}

    def gather(k, stage):
        order = ORDERS[k % len(ORDERS)]
        done, axis = order[:stage], order[stage]
        part = xbuf.at[
            k,
            core,
            slice(None) if "y" in done else y,
            slice(None) if "z" in done else z,
            slice(None) if "x" in done else row,
        ]
        return [
            remote(part, part, g_send.at[k, first_sem[axis] + i], g_recv.at[k, first_sem[axis] + i], peer)
            for i, peer in enumerate(peers[axis])
        ]

    started = []

    def start(copies):
        for copy in copies:
            copy.start()
            started.append(copy)

    def arrived(copies):
        for copy in copies:
            copy.wait_recv()

    def pass_on(k, stage):
        arrived(gather(k, stage - 1))
        start(gather(k, stage))

    for k in range(nk):
        start(gather(k, 0))
    for k in range(nk):
        pass_on(k, 1)

    member = ids_ref[...] == col
    hit_row = jnp.sum(member.astype(jnp.float32), axis=0, keepdims=True)
    weight_row = jnp.sum(jnp.where(member, weights_ref[...], 0.0), axis=0, keepdims=True)
    place = lax.broadcasted_iota(jnp.int32, (tokens, tokens), 0)
    other = lax.broadcasted_iota(jnp.int32, (tokens, tokens), 1)
    group = tokens // ROWS
    token = (
        ((place // 4) % 2) * group
        + ((place // 8) % 4) * 16
        + ((place // 32) % 2) * 8
        + (place // 64) * 4
        + place % 4
    )
    earlier = (other < token) & (other // group == token // group)
    rank = jnp.sum(jnp.where(earlier, hit_row, 0.0), axis=1, keepdims=True)
    same = other == token
    hit = jnp.sum(jnp.where(same, hit_row, 0.0), axis=1, keepdims=True)
    weight = jnp.sum(jnp.where(same, weight_row, 0.0), axis=1, keepdims=True)
    limit = capacity_ref[col].astype(jnp.float32)
    combine = jnp.where((hit > 0.5) & (rank < limit), weight, 0.0)
    combine = combine.astype(jnp.bfloat16).astype(jnp.float32)

    def send_hidden(h):
        part = hid.at[row, h]
        return [remote(part, part, h_send.at[h], h_recv.at[h], x_peer)]

    def product(k, part, first, count):
        return lax.dot_general(
            wgu[part, first : first + count, k * kc : (k + 1) * kc],
            x2d[k],
            (((1,), (1,)), ((), ())),
            preferred_element_type=jnp.float32,
        )

    for step in range(nk + 2):
        if step < nk:
            pass_on(step, 2)
        if 1 <= step <= nk:
            pass_on(step - 1, 3)
        if step < 2:
            continue
        k = step - 2
        arrived(gather(k, 3))
        block = xbuf[k].reshape(tokens // tok_dev, tok_dev, kc).astype(jnp.float32)
        x2d[k] = block.reshape(tokens, kc).astype(jnp.bfloat16)
        load_gu(k).wait()
        if k < nk - 1:
            for part in range(2):
                term = product(k, part, 0, hidden)
                acc[part] = term if k == 0 else acc[part] + term
            continue
        for h in range(tiles):
            rows = slice(h * TILE, (h + 1) * TILE)
            gate = acc[0, rows] + product(k, 0, h * TILE, TILE)
            up = acc[1, rows] + product(k, 1, h * TILE, TILE)
            act = gate / (1.0 + jnp.exp(-gate)) * up
            hid[row, h] = act.T.astype(jnp.bfloat16)
            start(send_hidden(h))

    def down_part(n, side):
        total = None
        for h in range(tiles):
            rows = pl.ds(pl.multiple_of(side * hidden + h * TILE, TILE), TILE)
            term = jnp.dot(
                hid[side, h],
                wd[rows, n * nc : (n + 1) * nc],
                preferred_element_type=jnp.float32,
            )
            total = term if total is None else total + term
        return total

    def reduce_1(n):
        return [remote(r1_out.at[n], r1_in.at[n], r_send.at[n, 0], r_recv.at[n, 0], core_peer)]

    def reduce_2(n):
        return [remote(r2_out.at[n], r2_in.at[n], r_send.at[n, 1], r_recv.at[n, 1], y_peer)]

    def reduce_3(n):
        return [
            remote(
                r3_out.at[n, z_places[i]],
                r3_in.at[n, i],
                r_send.at[n, 2 + i],
                r_recv.at[n, 2 + i],
                z_peers[i],
            )
            for i in range(ZS - 1)
        ]

    def reduce_4(n):
        return [
            remote(p3.at[n, 1 - row], r4_in.at[n], r_send.at[n, 5], r_recv.at[n, 5], x_peer)
        ]

    def after_core(n):
        arrived(reduce_1(n))
        both = zf[n, core] + r1_in[n].astype(jnp.float32)
        p1[n] = both.reshape(p1.shape[1:])
        r2_out[n] = p1[n, 1 - y].astype(jnp.bfloat16)
        start(reduce_2(n))

    def after_y(n):
        arrived(reduce_2(n))
        both = p1[n, y] + r2_in[n].astype(jnp.float32)
        p2[n] = both.reshape(p2.shape[1:])
        r3_out[n] = p2[n].astype(jnp.bfloat16)
        start(reduce_3(n))

    def after_z(n):
        arrived(reduce_3(n))
        total = p2[n, z]
        for i in range(ZS - 1):
            total = total + r3_in[n, i].astype(jnp.float32)
        p3[n, 0] = total[:tok_dev].astype(jnp.bfloat16)
        p3[n, 1] = total[tok_dev:].astype(jnp.bfloat16)
        start(reduce_4(n))

    for n in range(nr):
        load_d(n).wait()
        yacc[n] = down_part(n, row)
    for h in range(tiles):
        arrived(send_hidden(h))
    for n in range(nr + 3):
        if n < nr:
            total = (yacc[n] + down_part(n, 1 - row)).astype(jnp.bfloat16)
            scaled = total.astype(jnp.float32) * combine
            zf[n] = scaled.reshape(zf.shape[1:])
            r1_out[n] = zf[n, 1 - core].astype(jnp.bfloat16)
            start(reduce_1(n))
        if 1 <= n <= nr:
            after_core(n - 1)
        if 2 <= n <= nr + 1:
            after_y(n - 2)
        if n >= 3:
            after_z(n - 3)
    for n in range(nr):
        mine = pl.ds(pl.multiple_of(row * half + n * nc, 128), nc)
        theirs = pl.ds(pl.multiple_of((1 - row) * half + n * nc, 128), nc)
        out_ref[:, mine] = p3[n, row]
        arrived(reduce_4(n))
        out_ref[:, theirs] = r4_in[n]
    for copy in started:
        copy.wait_send()


def fused(tokens, gate_up, down, expert_ids, gate_weights, capacity):
    nk, nr = 2, 2
    tok_dev, width = tokens.shape
    total = expert_ids.shape[0]
    hidden = gate_up.shape[2]
    half = down.shape[2]
    kc, nc = width // nk, half // nr
    tiles = hidden // TILE
    vmem = pl.BlockSpec(memory_space=pltpu.VMEM)
    hbm = pl.BlockSpec(memory_space=pl.ANY)
    bf16, f32 = jnp.bfloat16, jnp.float32
    per_core, per_y, per_z = total // CORES, total // (CORES * YS), total // (CORES * YS * ZS)
    dma = pltpu.SemaphoreType.DMA
    return pl.pallas_call(
        functools.partial(fused_kernel, nk, nr),
        out_shape=jax.ShapeDtypeStruct(tokens.shape, bf16),
        in_specs=[vmem, vmem, vmem, pl.BlockSpec(memory_space=pltpu.SMEM), hbm, hbm],
        out_specs=vmem,
        scratch_shapes=[
            pltpu.VMEM((2, hidden, width), bf16),
            pltpu.VMEM((ROWS * hidden, half), bf16),
            pltpu.VMEM((nk, CORES, YS, ZS, ROWS, tok_dev, kc), bf16),
            pltpu.VMEM((nk, total, kc), bf16),
            pltpu.VMEM((2, hidden, total), f32),
            pltpu.VMEM((ROWS, tiles, total, TILE), bf16),
            pltpu.VMEM((nr, total, nc), f32),
            pltpu.VMEM((nr, CORES, per_core, nc), f32),
            pltpu.VMEM((nr, per_core, nc), bf16),
            pltpu.VMEM((nr, per_core, nc), bf16),
            pltpu.VMEM((nr, YS, per_y, nc), f32),
            pltpu.VMEM((nr, per_y, nc), bf16),
            pltpu.VMEM((nr, per_y, nc), bf16),
            pltpu.VMEM((nr, ZS, per_z, nc), f32),
            pltpu.VMEM((nr, ZS, per_z, nc), bf16),
            pltpu.VMEM((nr, ZS - 1, per_z, nc), bf16),
            pltpu.VMEM((nr, ROWS, tok_dev, nc), bf16),
            pltpu.VMEM((nr, tok_dev, nc), bf16),
            dma((nk + nr,)),
            dma((nk, 6)),
            dma((nk, 6)),
            dma((tiles,)),
            dma((tiles,)),
            dma((nr, 6)),
            dma((nr, 6)),
        ],
        compiler_params=pltpu.CompilerParams(
            collective_id=0, has_side_effects=True, vmem_limit_bytes=56 * 1024 * 1024
        ),
        cost_estimate=pl.CostEstimate(
            flops=6 * total * hidden * width,
            bytes_accessed=2 * (gate_up.size + down.size),
            transcendentals=total * hidden,
        ),
    )(tokens, expert_ids.T, gate_weights.T, capacity, gate_up, down)


def expert_slots(expert_ids, gate_weights, capacity, expert, block_rows, slot_cap):
    total_rows = expert_ids.shape[0]
    member = expert_ids == expert
    hit_count = jnp.sum(member.astype(jnp.int32), axis=1)
    grouped = hit_count.reshape(total_rows // block_rows, block_rows)
    rank_in = (jnp.cumsum(grouped, axis=1) - grouped).reshape(total_rows)
    cap_here = lax.dynamic_index_in_dim(capacity, expert, 0, keepdims=False)
    usable = (hit_count > 0) & (rank_in < cap_here)
    weights = jnp.sum(jnp.where(member, gate_weights, 0.0), axis=1)
    groups = jnp.arange(total_rows, dtype=jnp.int32) // block_rows
    slot_ids = jnp.where(usable, groups * slot_cap + rank_in, -1)
    return (slot_ids, weights)


def local(tokens, gate_up, down, expert_ids, gate_weights, capacity):
    col_count = lax.axis_size("col")
    row_count = lax.axis_size("row")
    col_index = lax.axis_index("col")
    row_index = lax.axis_index("row")
    tok_dev = tokens.shape[0]
    block_rows = col_count * tok_dev
    slot_cap = min(3 * tok_dev * TOP // 2, block_rows)
    slot_count = row_count * slot_cap
    total_rows = expert_ids.shape[0]
    slot_ids, weights = expert_slots(
        expert_ids, gate_weights, capacity, col_index, block_rows, slot_cap
    )
    group_tokens = lax.all_gather(tokens, "col", axis=0, tiled=True)
    local_slots = (
        lax.dynamic_slice_in_dim(slot_ids, row_index * block_rows, block_rows)
        - row_index * slot_cap
    )
    cap_index = jnp.arange(slot_cap, dtype=jnp.int32)
    select = (cap_index[:, None] == local_slots[None, :]).astype(jnp.bfloat16)
    picked = jnp.dot(select, group_tokens, preferred_element_type=jnp.float32).astype(jnp.bfloat16)
    w_gate = gate_up[0, 0]
    w_up = gate_up[0, 1]
    contract = (((1,), (1,)), ((), ()))
    piece = lax.all_gather(picked, "row", axis=0, tiled=True)
    gate_part = lax.dot_general(piece, w_gate, contract, preferred_element_type=jnp.float32)
    up_part = lax.dot_general(piece, w_up, contract, preferred_element_type=jnp.float32)
    hidden = (jax.nn.silu(gate_part) * up_part).astype(jnp.bfloat16)
    w_down = down[0]
    outputs = jnp.dot(
        lax.all_gather(hidden, "row", axis=1, tiled=True),
        w_down,
        preferred_element_type=jnp.float32,
    ).astype(jnp.bfloat16)

    def by_column(values):
        return values.reshape(row_count, col_count, tok_dev).transpose(1, 0, 2).reshape(total_rows)

    column_slots = by_column(slot_ids)
    column_weights = by_column(weights)
    slot_index = jnp.arange(slot_count, dtype=jnp.int32)
    combine = jnp.where(
        column_slots[:, None] == slot_index[None, :], column_weights[:, None], 0.0
    ).astype(jnp.bfloat16)
    summed = lax.psum_scatter(
        jnp.dot(combine, outputs, preferred_element_type=jnp.float32),
        "col",
        scatter_dimension=0,
        tiled=True,
    )
    own_rows = lax.all_to_all(
        summed.astype(jnp.bfloat16), "row", split_axis=0, concat_axis=1, tiled=True
    ).astype(summed.dtype)
    return own_rows.astype(jnp.bfloat16)


def solution(mesh):
    in_specs = (
        P(("row", "col"), None),
        P("col", None, "row", None),
        P("col", None, "row"),
        P(),
        P(),
        P(),
    )
    out_specs = P(("row", "col"), None)
    small = mesh.shape["row"] == ROWS and mesh.shape["col"] == CORES * YS * ZS
    return jax.shard_map(
        fused if small else local, mesh=mesh, in_specs=in_specs, out_specs=out_specs, check_vma=False
    )
```

```python
import functools

import jax
import jax.numpy as jnp
from jax import lax
from jax.experimental import pallas as pl
from jax.experimental.pallas import tpu as pltpu
from jax.sharding import PartitionSpec as P

TOP = 8
MESH = pl.DeviceIdType.MESH
CORES, YS, ZS, ROWS = 2, 2, 4, 2
ORDERS = ("xzyc", "yzxc")
TILE = 256


def fused_kernel(
    nk,
    nr,
    tokens_ref,
    ids_ref,
    weights_ref,
    capacity_ref,
    gate_up_ref,
    down_ref,
    out_ref,
    wgu,
    wd,
    xbuf,
    x2d,
    acc,
    hid,
    yacc,
    zf,
    r1_out,
    r1_in,
    p1,
    r2_out,
    r2_in,
    p2,
    r3_out,
    r3_in,
    p3,
    r4_in,
    load_sem,
    g_send,
    g_recv,
    h_send,
    h_recv,
    r_send,
    r_recv,
):
    row = lax.axis_index("row")
    col = lax.axis_index("col")
    core = col % CORES
    y = (col // CORES) % YS
    z = col // (CORES * YS)
    tok_dev, width = tokens_ref.shape
    kc = width // nk
    tokens = x2d.shape[1]
    half = down_ref.shape[2]
    nc = half // nr
    hidden = gate_up_ref.shape[2]
    tiles = hidden // TILE

    x_peer = (1 - row, col)
    y_peer = (row, z * 4 + (1 - y) * 2 + core)
    core_peer = (row, z * 4 + y * 2 + 1 - core)
    z_places = (z + 1 - 2 * (z % 2), (z + 2) % ZS, ZS - 1 - z)
    z_peers = [(row, place * 4 + y * 2 + core) for place in z_places]

    def load_gu(k):
        columns = pl.ds(k * kc, kc)
        return pltpu.make_async_copy(
            gate_up_ref.at[0, :, :, columns], wgu.at[:, :, columns], load_sem.at[k]
        )

    def load_d(n):
        columns = pl.ds(n * nc, nc)
        return pltpu.make_async_copy(
            down_ref.at[0, :, columns], wd.at[:, columns], load_sem.at[nk + n]
        )

    for k in range(nk):
        load_gu(k).start()
    for n in range(nr):
        load_d(n).start()

    barrier = pltpu.get_barrier_semaphore()
    for peer in [x_peer, y_peer, core_peer] + z_peers:
        pl.semaphore_signal(barrier, inc=1, device_id=peer, device_id_type=MESH)
    for k in range(nk):
        xbuf[k, core, y, z, row] = tokens_ref[:, k * kc : (k + 1) * kc]
    pl.semaphore_wait(barrier, 6)

    def remote(src, dst, send, recv, peer):
        return pltpu.make_async_remote_copy(
            src_ref=src,
            dst_ref=dst,
            send_sem=send,
            recv_sem=recv,
            device_id=peer,
            device_id_type=MESH,
        )

    peers = {"x": [x_peer], "z": z_peers, "y": [y_peer], "c": [core_peer]}
    first_sem = {"x": 0, "z": 1, "y": 4, "c": 5}

    def gather(k, stage):
        order = ORDERS[k % len(ORDERS)]
        done, axis = order[:stage], order[stage]
        part = xbuf.at[
            k,
            core,
            slice(None) if "y" in done else y,
            slice(None) if "z" in done else z,
            slice(None) if "x" in done else row,
        ]
        return [
            remote(part, part, g_send.at[k, first_sem[axis] + i], g_recv.at[k, first_sem[axis] + i], peer)
            for i, peer in enumerate(peers[axis])
        ]

    started = []

    def start(copies):
        for copy in copies:
            copy.start()
            started.append(copy)

    def arrived(copies):
        for copy in copies:
            copy.wait_recv()

    def pass_on(k, stage):
        arrived(gather(k, stage - 1))
        start(gather(k, stage))

    for k in range(nk):
        start(gather(k, 0))
    for k in range(nk):
        pass_on(k, 1)

    member = ids_ref[...] == col
    hit_row = jnp.sum(member.astype(jnp.float32), axis=0, keepdims=True)
    weight_row = jnp.sum(jnp.where(member, weights_ref[...], 0.0), axis=0, keepdims=True)
    place = lax.broadcasted_iota(jnp.int32, (tokens, tokens), 0)
    other = lax.broadcasted_iota(jnp.int32, (tokens, tokens), 1)
    group = tokens // ROWS
    token = (
        ((place // 4) % 2) * group
        + ((place // 8) % 4) * 16
        + ((place // 32) % 2) * 8
        + (place // 64) * 4
        + place % 4
    )
    earlier = (other < token) & (other // group == token // group)
    rank = jnp.sum(jnp.where(earlier, hit_row, 0.0), axis=1, keepdims=True)
    same = other == token
    hit = jnp.sum(jnp.where(same, hit_row, 0.0), axis=1, keepdims=True)
    weight = jnp.sum(jnp.where(same, weight_row, 0.0), axis=1, keepdims=True)
    limit = capacity_ref[col].astype(jnp.float32)
    combine = jnp.where((hit > 0.5) & (rank < limit), weight, 0.0)
    combine = combine.astype(jnp.bfloat16).astype(jnp.float32)

    def send_hidden(h):
        part = hid.at[row, h]
        return [remote(part, part, h_send.at[h], h_recv.at[h], x_peer)]

    def product(k, part, first, count):
        return lax.dot_general(
            wgu[part, first : first + count, k * kc : (k + 1) * kc],
            x2d[k],
            (((1,), (1,)), ((), ())),
            preferred_element_type=jnp.float32,
        )

    for k in range(nk):
        pass_on(k, 2)
        if k >= 2:
            pass_on(k - 2, 3)
    for k in range(nk):
        if k == 0:
            pass_on(nk - 2, 3)
        if k == 1:
            pass_on(nk - 1, 3)
        arrived(gather(k, 3))
        block = xbuf[k].reshape(tokens // tok_dev, tok_dev, kc).astype(jnp.float32)
        x2d[k] = block.reshape(tokens, kc).astype(jnp.bfloat16)
        load_gu(k).wait()
        if k < nk - 1:
            for part in range(2):
                term = product(k, part, 0, hidden)
                acc[part] = term if k == 0 else acc[part] + term
            continue
        for h in range(tiles):
            rows = slice(h * TILE, (h + 1) * TILE)
            gate = acc[0, rows] + product(k, 0, h * TILE, TILE)
            up = acc[1, rows] + product(k, 1, h * TILE, TILE)
            act = gate / (1.0 + jnp.exp(-gate)) * up
            hid[row, h] = act.T.astype(jnp.bfloat16)
            start(send_hidden(h))

    def down_part(n, side):
        total = None
        for h in range(tiles):
            rows = pl.ds(pl.multiple_of(side * hidden + h * TILE, TILE), TILE)
            term = jnp.dot(
                hid[side, h],
                wd[rows, n * nc : (n + 1) * nc],
                preferred_element_type=jnp.float32,
            )
            total = term if total is None else total + term
        return total

    def reduce_1(n):
        return [remote(r1_out.at[n], r1_in.at[n], r_send.at[n, 0], r_recv.at[n, 0], core_peer)]

    def reduce_2(n):
        return [remote(r2_out.at[n], r2_in.at[n], r_send.at[n, 1], r_recv.at[n, 1], y_peer)]

    def reduce_3(n):
        return [
            remote(
                r3_out.at[n, z_places[i]],
                r3_in.at[n, i],
                r_send.at[n, 2 + i],
                r_recv.at[n, 2 + i],
                z_peers[i],
            )
            for i in range(ZS - 1)
        ]

    def reduce_4(n):
        return [
            remote(p3.at[n, 1 - row], r4_in.at[n], r_send.at[n, 5], r_recv.at[n, 5], x_peer)
        ]

    def after_core(n):
        arrived(reduce_1(n))
        both = zf[n, core] + r1_in[n].astype(jnp.float32)
        p1[n] = both.reshape(p1.shape[1:])
        r2_out[n] = p1[n, 1 - y].astype(jnp.bfloat16)
        start(reduce_2(n))

    def after_y(n):
        arrived(reduce_2(n))
        both = p1[n, y] + r2_in[n].astype(jnp.float32)
        p2[n] = both.reshape(p2.shape[1:])
        r3_out[n] = p2[n].astype(jnp.bfloat16)
        start(reduce_3(n))

    def after_z(n):
        arrived(reduce_3(n))
        total = p2[n, z]
        for i in range(ZS - 1):
            total = total + r3_in[n, i].astype(jnp.float32)
        p3[n, 0] = total[:tok_dev].astype(jnp.bfloat16)
        p3[n, 1] = total[tok_dev:].astype(jnp.bfloat16)
        start(reduce_4(n))

    for n in range(nr):
        load_d(n).wait()
        yacc[n] = down_part(n, row)
    for h in range(tiles):
        arrived(send_hidden(h))
    for n in range(nr):
        total = (yacc[n] + down_part(n, 1 - row)).astype(jnp.bfloat16)
        scaled = total.astype(jnp.float32) * combine
        zf[n] = scaled.reshape(zf.shape[1:])
        r1_out[n] = zf[n, 1 - core].astype(jnp.bfloat16)
        start(reduce_1(n))
        if n >= 2:
            after_core(n - 2)
    for n in range(nr - 2, nr):
        after_core(n)
    for n in range(nr):
        after_y(n)
    for n in range(nr):
        after_z(n)
    for n in range(nr):
        mine = pl.ds(pl.multiple_of(row * half + n * nc, 128), nc)
        theirs = pl.ds(pl.multiple_of((1 - row) * half + n * nc, 128), nc)
        out_ref[:, mine] = p3[n, row]
        arrived(reduce_4(n))
        out_ref[:, theirs] = r4_in[n]
    for copy in started:
        copy.wait_send()


def fused(tokens, gate_up, down, expert_ids, gate_weights, capacity):
    nk, nr = 4, 4
    tok_dev, width = tokens.shape
    total = expert_ids.shape[0]
    hidden = gate_up.shape[2]
    half = down.shape[2]
    kc, nc = width // nk, half // nr
    tiles = hidden // TILE
    vmem = pl.BlockSpec(memory_space=pltpu.VMEM)
    hbm = pl.BlockSpec(memory_space=pl.ANY)
    bf16, f32 = jnp.bfloat16, jnp.float32
    per_core, per_y, per_z = total // CORES, total // (CORES * YS), total // (CORES * YS * ZS)
    dma = pltpu.SemaphoreType.DMA
    return pl.pallas_call(
        functools.partial(fused_kernel, nk, nr),
        out_shape=jax.ShapeDtypeStruct(tokens.shape, bf16),
        in_specs=[vmem, vmem, vmem, pl.BlockSpec(memory_space=pltpu.SMEM), hbm, hbm],
        out_specs=vmem,
        scratch_shapes=[
            pltpu.VMEM((2, hidden, width), bf16),
            pltpu.VMEM((ROWS * hidden, half), bf16),
            pltpu.VMEM((nk, CORES, YS, ZS, ROWS, tok_dev, kc), bf16),
            pltpu.VMEM((nk, total, kc), bf16),
            pltpu.VMEM((2, hidden, total), f32),
            pltpu.VMEM((ROWS, tiles, total, TILE), bf16),
            pltpu.VMEM((nr, total, nc), f32),
            pltpu.VMEM((nr, CORES, per_core, nc), f32),
            pltpu.VMEM((nr, per_core, nc), bf16),
            pltpu.VMEM((nr, per_core, nc), bf16),
            pltpu.VMEM((nr, YS, per_y, nc), f32),
            pltpu.VMEM((nr, per_y, nc), bf16),
            pltpu.VMEM((nr, per_y, nc), bf16),
            pltpu.VMEM((nr, ZS, per_z, nc), f32),
            pltpu.VMEM((nr, ZS, per_z, nc), bf16),
            pltpu.VMEM((nr, ZS - 1, per_z, nc), bf16),
            pltpu.VMEM((nr, ROWS, tok_dev, nc), bf16),
            pltpu.VMEM((nr, tok_dev, nc), bf16),
            dma((nk + nr,)),
            dma((nk, 6)),
            dma((nk, 6)),
            dma((tiles,)),
            dma((tiles,)),
            dma((nr, 6)),
            dma((nr, 6)),
        ],
        compiler_params=pltpu.CompilerParams(
            collective_id=0, has_side_effects=True, vmem_limit_bytes=56 * 1024 * 1024
        ),
        cost_estimate=pl.CostEstimate(
            flops=6 * total * hidden * width,
            bytes_accessed=2 * (gate_up.size + down.size),
            transcendentals=total * hidden,
        ),
    )(tokens, expert_ids.T, gate_weights.T, capacity, gate_up, down)


def expert_slots(expert_ids, gate_weights, capacity, expert, block_rows, slot_cap):
    total_rows = expert_ids.shape[0]
    member = expert_ids == expert
    hit_count = jnp.sum(member.astype(jnp.int32), axis=1)
    grouped = hit_count.reshape(total_rows // block_rows, block_rows)
    rank_in = (jnp.cumsum(grouped, axis=1) - grouped).reshape(total_rows)
    cap_here = lax.dynamic_index_in_dim(capacity, expert, 0, keepdims=False)
    usable = (hit_count > 0) & (rank_in < cap_here)
    weights = jnp.sum(jnp.where(member, gate_weights, 0.0), axis=1)
    groups = jnp.arange(total_rows, dtype=jnp.int32) // block_rows
    slot_ids = jnp.where(usable, groups * slot_cap + rank_in, -1)
    return (slot_ids, weights)


def local(tokens, gate_up, down, expert_ids, gate_weights, capacity):
    col_count = lax.axis_size("col")
    row_count = lax.axis_size("row")
    col_index = lax.axis_index("col")
    row_index = lax.axis_index("row")
    tok_dev = tokens.shape[0]
    block_rows = col_count * tok_dev
    slot_cap = min(3 * tok_dev * TOP // 2, block_rows)
    slot_count = row_count * slot_cap
    total_rows = expert_ids.shape[0]
    slot_ids, weights = expert_slots(
        expert_ids, gate_weights, capacity, col_index, block_rows, slot_cap
    )
    group_tokens = lax.all_gather(tokens, "col", axis=0, tiled=True)
    local_slots = (
        lax.dynamic_slice_in_dim(slot_ids, row_index * block_rows, block_rows)
        - row_index * slot_cap
    )
    cap_index = jnp.arange(slot_cap, dtype=jnp.int32)
    select = (cap_index[:, None] == local_slots[None, :]).astype(jnp.bfloat16)
    picked = jnp.dot(select, group_tokens, preferred_element_type=jnp.float32).astype(jnp.bfloat16)
    w_gate = gate_up[0, 0]
    w_up = gate_up[0, 1]
    contract = (((1,), (1,)), ((), ()))
    piece = lax.all_gather(picked, "row", axis=0, tiled=True)
    gate_part = lax.dot_general(piece, w_gate, contract, preferred_element_type=jnp.float32)
    up_part = lax.dot_general(piece, w_up, contract, preferred_element_type=jnp.float32)
    hidden = (jax.nn.silu(gate_part) * up_part).astype(jnp.bfloat16)
    w_down = down[0]
    outputs = jnp.dot(
        lax.all_gather(hidden, "row", axis=1, tiled=True),
        w_down,
        preferred_element_type=jnp.float32,
    ).astype(jnp.bfloat16)

    def by_column(values):
        return values.reshape(row_count, col_count, tok_dev).transpose(1, 0, 2).reshape(total_rows)

    column_slots = by_column(slot_ids)
    column_weights = by_column(weights)
    slot_index = jnp.arange(slot_count, dtype=jnp.int32)
    combine = jnp.where(
        column_slots[:, None] == slot_index[None, :], column_weights[:, None], 0.0
    ).astype(jnp.bfloat16)
    summed = lax.psum_scatter(
        jnp.dot(combine, outputs, preferred_element_type=jnp.float32),
        "col",
        scatter_dimension=0,
        tiled=True,
    )
    own_rows = lax.all_to_all(
        summed.astype(jnp.bfloat16), "row", split_axis=0, concat_axis=1, tiled=True
    ).astype(summed.dtype)
    return own_rows.astype(jnp.bfloat16)


def solution(mesh):
    in_specs = (
        P(("row", "col"), None),
        P("col", None, "row", None),
        P("col", None, "row"),
        P(),
        P(),
        P(),
    )
    out_specs = P(("row", "col"), None)
    small = mesh.shape["row"] == ROWS and mesh.shape["col"] == CORES * YS * ZS
    return jax.shard_map(
        fused if small else local, mesh=mesh, in_specs=in_specs, out_specs=out_specs, check_vma=False
    )
```

```python
import functools

import jax
import jax.numpy as jnp
from jax import lax
from jax.experimental import pallas as pl
from jax.experimental.pallas import tpu as pltpu
from jax.sharding import PartitionSpec as P

TOP = 8
MESH = pl.DeviceIdType.MESH
CORES, YS, ZS, ROWS = 2, 2, 4, 2
ORDERS = ("xzyc", "yzxc", "zxyc", "zyxc")
TILE = 256


def fused_kernel(
    nk,
    nr,
    tokens_ref,
    ids_ref,
    weights_ref,
    capacity_ref,
    gate_up_ref,
    down_ref,
    out_ref,
    wgu,
    wd,
    xbuf,
    x2d,
    acc,
    hid,
    yacc,
    zf,
    r1_out,
    r1_in,
    p1,
    r2_out,
    r2_in,
    p2,
    r3_out,
    r3_in,
    p3,
    r4_in,
    load_sem,
    g_send,
    g_recv,
    h_send,
    h_recv,
    r_send,
    r_recv,
):
    row = lax.axis_index("row")
    col = lax.axis_index("col")
    core = col % CORES
    y = (col // CORES) % YS
    z = col // (CORES * YS)
    tok_dev, width = tokens_ref.shape
    kc = width // nk
    tokens = x2d.shape[1]
    half = down_ref.shape[2]
    nc = half // nr
    hidden = gate_up_ref.shape[2]
    tiles = hidden // TILE

    x_peer = (1 - row, col)
    y_peer = (row, z * 4 + (1 - y) * 2 + core)
    core_peer = (row, z * 4 + y * 2 + 1 - core)
    z_places = (z + 1 - 2 * (z % 2), (z + 2) % ZS, ZS - 1 - z)
    z_peers = [(row, place * 4 + y * 2 + core) for place in z_places]

    def load_gu(k):
        columns = pl.ds(k * kc, kc)
        return pltpu.make_async_copy(
            gate_up_ref.at[0, :, :, columns], wgu.at[:, :, columns], load_sem.at[k]
        )

    def load_d(n):
        columns = pl.ds(n * nc, nc)
        return pltpu.make_async_copy(
            down_ref.at[0, :, columns], wd.at[:, columns], load_sem.at[nk + n]
        )

    for k in range(nk):
        load_gu(k).start()
    for n in range(nr):
        load_d(n).start()

    barrier = pltpu.get_barrier_semaphore()
    for peer in [x_peer, y_peer, core_peer] + z_peers:
        pl.semaphore_signal(barrier, inc=1, device_id=peer, device_id_type=MESH)
    for k in range(nk):
        xbuf[k, core, y, z, row] = tokens_ref[:, k * kc : (k + 1) * kc]
    pl.semaphore_wait(barrier, 6)

    def remote(src, dst, send, recv, peer):
        return pltpu.make_async_remote_copy(
            src_ref=src,
            dst_ref=dst,
            send_sem=send,
            recv_sem=recv,
            device_id=peer,
            device_id_type=MESH,
        )

    peers = {"x": [x_peer], "z": z_peers, "y": [y_peer], "c": [core_peer]}
    first_sem = {"x": 0, "z": 1, "y": 4, "c": 5}

    def gather(k, stage):
        order = ORDERS[k % len(ORDERS)]
        done, axis = order[:stage], order[stage]
        part = xbuf.at[
            k,
            core,
            slice(None) if "y" in done else y,
            slice(None) if "z" in done else z,
            slice(None) if "x" in done else row,
        ]
        return [
            remote(part, part, g_send.at[k, first_sem[axis] + i], g_recv.at[k, first_sem[axis] + i], peer)
            for i, peer in enumerate(peers[axis])
        ]

    started = []

    def start(copies):
        for copy in copies:
            copy.start()
            started.append(copy)

    def arrived(copies):
        for copy in copies:
            copy.wait_recv()

    def pass_on(k, stage):
        arrived(gather(k, stage - 1))
        start(gather(k, stage))

    for k in range(nk):
        start(gather(k, 0))
    for k in range(nk):
        pass_on(k, 1)

    member = ids_ref[...] == col
    hit_row = jnp.sum(member.astype(jnp.float32), axis=0, keepdims=True)
    weight_row = jnp.sum(jnp.where(member, weights_ref[...], 0.0), axis=0, keepdims=True)
    place = lax.broadcasted_iota(jnp.int32, (tokens, tokens), 0)
    other = lax.broadcasted_iota(jnp.int32, (tokens, tokens), 1)
    group = tokens // ROWS
    token = (
        ((place // 4) % 2) * group
        + ((place // 8) % 4) * 16
        + ((place // 32) % 2) * 8
        + (place // 64) * 4
        + place % 4
    )
    earlier = (other < token) & (other // group == token // group)
    rank = jnp.sum(jnp.where(earlier, hit_row, 0.0), axis=1, keepdims=True)
    same = other == token
    hit = jnp.sum(jnp.where(same, hit_row, 0.0), axis=1, keepdims=True)
    weight = jnp.sum(jnp.where(same, weight_row, 0.0), axis=1, keepdims=True)
    limit = capacity_ref[col].astype(jnp.float32)
    combine = jnp.where((hit > 0.5) & (rank < limit), weight, 0.0)
    combine = combine.astype(jnp.bfloat16).astype(jnp.float32)

    def send_hidden(h):
        part = hid.at[row, h]
        return [remote(part, part, h_send.at[h], h_recv.at[h], x_peer)]

    def product(k, part, first, count):
        return lax.dot_general(
            wgu[part, first : first + count, k * kc : (k + 1) * kc],
            x2d[k],
            (((1,), (1,)), ((), ())),
            preferred_element_type=jnp.float32,
        )

    for k in range(nk):
        pass_on(k, 2)
        if k >= 2:
            pass_on(k - 2, 3)
    for k in range(nk):
        if k == 0:
            pass_on(nk - 2, 3)
        if k == 1:
            pass_on(nk - 1, 3)
        arrived(gather(k, 3))
        block = xbuf[k].reshape(tokens // tok_dev, tok_dev, kc).astype(jnp.float32)
        x2d[k] = block.reshape(tokens, kc).astype(jnp.bfloat16)
        load_gu(k).wait()
        if k < nk - 1:
            for part in range(2):
                term = product(k, part, 0, hidden)
                acc[part] = term if k == 0 else acc[part] + term
            continue
        for h in range(tiles):
            rows = slice(h * TILE, (h + 1) * TILE)
            gate = acc[0, rows] + product(k, 0, h * TILE, TILE)
            up = acc[1, rows] + product(k, 1, h * TILE, TILE)
            act = gate / (1.0 + jnp.exp(-gate)) * up
            hid[row, h] = act.T.astype(jnp.bfloat16)
            start(send_hidden(h))

    def down_part(n, side):
        total = None
        for h in range(tiles):
            rows = pl.ds(pl.multiple_of(side * hidden + h * TILE, TILE), TILE)
            term = jnp.dot(
                hid[side, h],
                wd[rows, n * nc : (n + 1) * nc],
                preferred_element_type=jnp.float32,
            )
            total = term if total is None else total + term
        return total

    def reduce_1(n):
        return [remote(r1_out.at[n], r1_in.at[n], r_send.at[n, 0], r_recv.at[n, 0], core_peer)]

    def reduce_2(n):
        return [remote(r2_out.at[n], r2_in.at[n], r_send.at[n, 1], r_recv.at[n, 1], y_peer)]

    def reduce_3(n):
        return [
            remote(
                r3_out.at[n, z_places[i]],
                r3_in.at[n, i],
                r_send.at[n, 2 + i],
                r_recv.at[n, 2 + i],
                z_peers[i],
            )
            for i in range(ZS - 1)
        ]

    def reduce_4(n):
        return [
            remote(p3.at[n, 1 - row], r4_in.at[n], r_send.at[n, 5], r_recv.at[n, 5], x_peer)
        ]

    def after_core(n):
        arrived(reduce_1(n))
        both = zf[n, core] + r1_in[n].astype(jnp.float32)
        p1[n] = both.reshape(p1.shape[1:])
        r2_out[n] = p1[n, 1 - y].astype(jnp.bfloat16)
        start(reduce_2(n))

    def after_y(n):
        arrived(reduce_2(n))
        both = p1[n, y] + r2_in[n].astype(jnp.float32)
        p2[n] = both.reshape(p2.shape[1:])
        r3_out[n] = p2[n].astype(jnp.bfloat16)
        start(reduce_3(n))

    def after_z(n):
        arrived(reduce_3(n))
        total = p2[n, z]
        for i in range(ZS - 1):
            total = total + r3_in[n, i].astype(jnp.float32)
        p3[n, 0] = total[:tok_dev].astype(jnp.bfloat16)
        p3[n, 1] = total[tok_dev:].astype(jnp.bfloat16)
        start(reduce_4(n))

    for n in range(nr):
        load_d(n).wait()
        yacc[n] = down_part(n, row)
    for h in range(tiles):
        arrived(send_hidden(h))
    for n in range(nr):
        total = (yacc[n] + down_part(n, 1 - row)).astype(jnp.bfloat16)
        scaled = total.astype(jnp.float32) * combine
        zf[n] = scaled.reshape(zf.shape[1:])
        r1_out[n] = zf[n, 1 - core].astype(jnp.bfloat16)
        start(reduce_1(n))
        if n >= 2:
            after_core(n - 2)
    for n in range(nr - 2, nr):
        after_core(n)
    for n in range(nr):
        after_y(n)
    for n in range(nr):
        after_z(n)
    for n in range(nr):
        mine = pl.ds(pl.multiple_of(row * half + n * nc, 128), nc)
        theirs = pl.ds(pl.multiple_of((1 - row) * half + n * nc, 128), nc)
        out_ref[:, mine] = p3[n, row]
        arrived(reduce_4(n))
        out_ref[:, theirs] = r4_in[n]
    for copy in started:
        copy.wait_send()


def fused(tokens, gate_up, down, expert_ids, gate_weights, capacity):
    nk, nr = 4, 4
    tok_dev, width = tokens.shape
    total = expert_ids.shape[0]
    hidden = gate_up.shape[2]
    half = down.shape[2]
    kc, nc = width // nk, half // nr
    tiles = hidden // TILE
    vmem = pl.BlockSpec(memory_space=pltpu.VMEM)
    hbm = pl.BlockSpec(memory_space=pl.ANY)
    bf16, f32 = jnp.bfloat16, jnp.float32
    per_core, per_y, per_z = total // CORES, total // (CORES * YS), total // (CORES * YS * ZS)
    dma = pltpu.SemaphoreType.DMA
    return pl.pallas_call(
        functools.partial(fused_kernel, nk, nr),
        out_shape=jax.ShapeDtypeStruct(tokens.shape, bf16),
        in_specs=[vmem, vmem, vmem, pl.BlockSpec(memory_space=pltpu.SMEM), hbm, hbm],
        out_specs=vmem,
        scratch_shapes=[
            pltpu.VMEM((2, hidden, width), bf16),
            pltpu.VMEM((ROWS * hidden, half), bf16),
            pltpu.VMEM((nk, CORES, YS, ZS, ROWS, tok_dev, kc), bf16),
            pltpu.VMEM((nk, total, kc), bf16),
            pltpu.VMEM((2, hidden, total), f32),
            pltpu.VMEM((ROWS, tiles, total, TILE), bf16),
            pltpu.VMEM((nr, total, nc), f32),
            pltpu.VMEM((nr, CORES, per_core, nc), f32),
            pltpu.VMEM((nr, per_core, nc), bf16),
            pltpu.VMEM((nr, per_core, nc), bf16),
            pltpu.VMEM((nr, YS, per_y, nc), f32),
            pltpu.VMEM((nr, per_y, nc), bf16),
            pltpu.VMEM((nr, per_y, nc), bf16),
            pltpu.VMEM((nr, ZS, per_z, nc), f32),
            pltpu.VMEM((nr, ZS, per_z, nc), bf16),
            pltpu.VMEM((nr, ZS - 1, per_z, nc), bf16),
            pltpu.VMEM((nr, ROWS, tok_dev, nc), bf16),
            pltpu.VMEM((nr, tok_dev, nc), bf16),
            dma((nk + nr,)),
            dma((nk, 6)),
            dma((nk, 6)),
            dma((tiles,)),
            dma((tiles,)),
            dma((nr, 6)),
            dma((nr, 6)),
        ],
        compiler_params=pltpu.CompilerParams(
            collective_id=0, has_side_effects=True, vmem_limit_bytes=56 * 1024 * 1024
        ),
        cost_estimate=pl.CostEstimate(
            flops=6 * total * hidden * width,
            bytes_accessed=2 * (gate_up.size + down.size),
            transcendentals=total * hidden,
        ),
    )(tokens, expert_ids.T, gate_weights.T, capacity, gate_up, down)


def expert_slots(expert_ids, gate_weights, capacity, expert, block_rows, slot_cap):
    total_rows = expert_ids.shape[0]
    member = expert_ids == expert
    hit_count = jnp.sum(member.astype(jnp.int32), axis=1)
    grouped = hit_count.reshape(total_rows // block_rows, block_rows)
    rank_in = (jnp.cumsum(grouped, axis=1) - grouped).reshape(total_rows)
    cap_here = lax.dynamic_index_in_dim(capacity, expert, 0, keepdims=False)
    usable = (hit_count > 0) & (rank_in < cap_here)
    weights = jnp.sum(jnp.where(member, gate_weights, 0.0), axis=1)
    groups = jnp.arange(total_rows, dtype=jnp.int32) // block_rows
    slot_ids = jnp.where(usable, groups * slot_cap + rank_in, -1)
    return (slot_ids, weights)


def local(tokens, gate_up, down, expert_ids, gate_weights, capacity):
    col_count = lax.axis_size("col")
    row_count = lax.axis_size("row")
    col_index = lax.axis_index("col")
    row_index = lax.axis_index("row")
    tok_dev = tokens.shape[0]
    block_rows = col_count * tok_dev
    slot_cap = min(3 * tok_dev * TOP // 2, block_rows)
    slot_count = row_count * slot_cap
    total_rows = expert_ids.shape[0]
    slot_ids, weights = expert_slots(
        expert_ids, gate_weights, capacity, col_index, block_rows, slot_cap
    )
    group_tokens = lax.all_gather(tokens, "col", axis=0, tiled=True)
    local_slots = (
        lax.dynamic_slice_in_dim(slot_ids, row_index * block_rows, block_rows)
        - row_index * slot_cap
    )
    cap_index = jnp.arange(slot_cap, dtype=jnp.int32)
    select = (cap_index[:, None] == local_slots[None, :]).astype(jnp.bfloat16)
    picked = jnp.dot(select, group_tokens, preferred_element_type=jnp.float32).astype(jnp.bfloat16)
    w_gate = gate_up[0, 0]
    w_up = gate_up[0, 1]
    contract = (((1,), (1,)), ((), ()))
    piece = lax.all_gather(picked, "row", axis=0, tiled=True)
    gate_part = lax.dot_general(piece, w_gate, contract, preferred_element_type=jnp.float32)
    up_part = lax.dot_general(piece, w_up, contract, preferred_element_type=jnp.float32)
    hidden = (jax.nn.silu(gate_part) * up_part).astype(jnp.bfloat16)
    w_down = down[0]
    outputs = jnp.dot(
        lax.all_gather(hidden, "row", axis=1, tiled=True),
        w_down,
        preferred_element_type=jnp.float32,
    ).astype(jnp.bfloat16)

    def by_column(values):
        return values.reshape(row_count, col_count, tok_dev).transpose(1, 0, 2).reshape(total_rows)

    column_slots = by_column(slot_ids)
    column_weights = by_column(weights)
    slot_index = jnp.arange(slot_count, dtype=jnp.int32)
    combine = jnp.where(
        column_slots[:, None] == slot_index[None, :], column_weights[:, None], 0.0
    ).astype(jnp.bfloat16)
    summed = lax.psum_scatter(
        jnp.dot(combine, outputs, preferred_element_type=jnp.float32),
        "col",
        scatter_dimension=0,
        tiled=True,
    )
    own_rows = lax.all_to_all(
        summed.astype(jnp.bfloat16), "row", split_axis=0, concat_axis=1, tiled=True
    ).astype(summed.dtype)
    return own_rows.astype(jnp.bfloat16)


def solution(mesh):
    in_specs = (
        P(("row", "col"), None),
        P("col", None, "row", None),
        P("col", None, "row"),
        P(),
        P(),
        P(),
    )
    out_specs = P(("row", "col"), None)
    small = mesh.shape["row"] == ROWS and mesh.shape["col"] == CORES * YS * ZS
    return jax.shard_map(
        fused if small else local, mesh=mesh, in_specs=in_specs, out_specs=out_specs, check_vma=False
    )
```
